32 devices in a mesh: shell: 4 (over z), sector: 8 (over y, x, core).
Axes of the slice: x: 2, y: 2, z: 4, core: 2. Of those that a mesh axis runs over, the one named last changes fastest.
Arguments:
- bricks: bfloat16 [4, 64, 32, 512], P('shell', 'sector'), may hold values from -6 to 6
- conv_w: bfloat16 [32, 864], replicated, may hold values from -0.21875 to 0.21875
- conv_b: float32 [32], replicated, may hold values from -3 to 3
- head_w1: bfloat16 [32, 64], replicated, may hold values from -1 to 1
- head_b1: float32 [64], replicated, may hold values from -3 to 3
- head_w2: float32 [64, 2], replicated, may hold values from -0.75 to 0.75
- queries: int32 [4, 64, 1024], P('shell', 'sector'), may hold values from -1 to 4095, as said below
- sample_src: int32 [4, 32768], P('shell', 'sector'), may hold values from 0 to 8191, as said below
- depth_target: float32 [4096], P('sector'), may hold values from 0.1 to 0.9
- inten_target: float32 [4096], P('sector'), may hold values from 0 to 1
- drop_label: int32 [4096], P('sector'), may hold values 0 or 1
Outputs:
- loss_mean: float32 [], replicated
- grad_conv_w: float32 [32, 864], replicated
- grad_conv_b: float32 [32], replicated
- grad_head_w1: float32 [32, 64], replicated
- grad_head_b1: float32 [64], replicated
- grad_head_w2: float32 [64, 2], replicated
- grad_bricks: bfloat16 [4, 64, 32, 512], P('shell', 'sector')
- ray_depth: float32 [4096], P('sector')
The draws below stay inside these ranges and needn't reach their ends.
Inputs may be any that keep to these rules, and one draw needn't show every extreme that they name: `queries`: entry of the buffer from a device of sector v to owner w: a cell address (brick of the owner times 512 plus cell) or -1 for an empty slot. Every sample of a device holds exactly one live slot, named by sample_src as w * 1024 + slot. In every shell one owner receives full buffers of 1024 from every sector. `sample_src`: A slot w * 1024 + slot of the sample's own device; distinct samples of a device have distinct slots.
All inputs are finite; a program needn't handle non-finite values. No bound on the sum of `drop_label` on one device may be relied on, other than what follows from the above.
Results may differ from the reference program's by a relative error of at most 0.0015.
The reference program's roundings to bfloat16 on the way count: a program that leaves them out, or rounds other values in their place, can miss the bound.
Values may be sent and summed in bfloat16 or wider, within the bound.
A program may use at most 192 MiB of HBM per device.

```python
import math
import jax
import jax.numpy as jnp
from jax import lax

CH = 32
HID = 64
SAMP = 8
RAY_DEV = 512
BRICK_DEV = 8
CAP = 1024
RAYS = 4096
BRICKS = 64
N_SHELL = 4
N_SECTOR = 8


def build_plan(base_key):
    per_device = RAY_DEV * SAMP
    rank_list = jnp.arange(per_device, dtype=jnp.int32)

    def one_device(shell_key, source):
        device_key = jax.random.fold_in(shell_key, source + 1000)
        busiest = jax.random.randint(shell_key, (), 0, N_SECTOR, dtype=jnp.int32)
        rank_order = jax.random.permutation(jax.random.fold_in(device_key, 1), per_device).astype(jnp.int32)
        spread = rank_list - CAP
        owner_rank = jnp.where(rank_list < CAP, busiest, (busiest + 1 + spread % (N_SECTOR - 1)) % N_SECTOR)
        drawn_pos = spread // (N_SECTOR - 1)
        other_pos = jnp.where(owner_rank == N_SECTOR - 1, CAP - 1 - drawn_pos, drawn_pos)
        position = jnp.where(rank_list < CAP, rank_list, other_pos)
        address = jax.random.randint(jax.random.fold_in(device_key, 2), (per_device,), 0, BRICK_DEV * 512, dtype=jnp.int32)
        address = address.at[0].set(BRICK_DEV * 512 - 1)
        slot_index = (owner_rank * CAP + position).astype(jnp.int32)
        sources = jnp.zeros((per_device,), jnp.int32).at[rank_order].set(slot_index)
        slot_table = jnp.full((N_SECTOR * CAP,), -1, jnp.int32).at[slot_index].set(address)
        return (slot_table.reshape(N_SECTOR, CAP), sources)

    def one_shell(shell_id):
        shell_key = jax.random.fold_in(base_key, shell_id)
        return jax.vmap(lambda source: one_device(shell_key, source))(jnp.arange(N_SECTOR, dtype=jnp.int32))
    tables, sources = jax.vmap(one_shell)(jnp.arange(N_SHELL, dtype=jnp.int32))
    return (tables.reshape(N_SHELL, N_SECTOR * N_SECTOR, CAP), sources.reshape(N_SHELL, N_SECTOR * per_device))


def draw_queries(key, part):
    return build_plan(jax.random.fold_in(key, 77))[0]


def draw_sample_src(key, part):
    return build_plan(jax.random.fold_in(key, 77))[1]


def touch_ends(entries, rng, low, high):
    index_at = [jax.random.randint(jax.random.fold_in(rng, axis), (), 0, length) for axis, length in enumerate(entries.shape)]
    main_axis = entries.shape.index(max(entries.shape))
    neighbour = index_at[:main_axis] + [(index_at[main_axis] + 1) % entries.shape[main_axis]] + index_at[main_axis + 1:]
    return entries.at[tuple(index_at)].set(low).at[tuple(neighbour)].set(high)


def block_levels(rng, dims, cuts, least, top_value):
    factor_of = 1.0
    for dim, blocks in cuts:
        draws = jax.random.uniform(jax.random.fold_in(jax.random.fold_in(rng, 6), dim), (blocks,), jnp.float32, least / len(cuts), top_value / len(cuts))
        factor_of = factor_of * jnp.repeat(jnp.exp(draws), dims[dim] // blocks).reshape((-1,) + (1,) * (len(dims) - 1 - dim))
    return factor_of


def gaussian(stream_key, shape, scale, reach, cuts=(), kind=jnp.bfloat16):
    gain = block_levels(stream_key, shape, cuts, -0.22, 0.18) if cuts else 1.0
    values = jax.random.normal(stream_key, shape, jnp.float32) * scale * gain
    return jnp.minimum(jnp.maximum(values, -reach), reach).astype(kind)


def setup_inputs(seed: int = 0) -> dict:
    streams_of = jax.random.split(jax.random.key(seed), 12)
    return {
        "bricks": gaussian(streams_of[0], (N_SHELL, BRICKS, CH, 512), 1.0, 6.0, ((0, 4), (1, 8))),
        "conv_w": gaussian(streams_of[1], (CH, 27 * CH), (27 * CH) ** -0.5, 0.21875),
        "conv_b": gaussian(streams_of[2], (CH,), 0.5, 3.0, (), jnp.float32),
        "head_w1": gaussian(streams_of[3], (CH, HID), CH ** -0.5, 1.0),
        "head_b1": gaussian(streams_of[4], (HID,), 0.5, 3.0, (), jnp.float32),
        "head_w2": gaussian(streams_of[5], (HID, 2), HID ** -0.5, 0.75, (), jnp.float32),
        "queries": draw_queries(jax.random.fold_in(streams_of[11], 71), 0),
        "sample_src": draw_sample_src(jax.random.fold_in(streams_of[11], 71), 0),
        "depth_target": jnp.clip(0.1 + 0.79999997 * jax.random.uniform(streams_of[8], (RAYS,), jnp.float32) ** block_levels(streams_of[8], (RAYS,), ((0, 8),), -0.2, 0.2), 0.1, 0.9),
        "inten_target": jnp.clip(1.0 * jax.random.uniform(streams_of[9], (RAYS,), jnp.float32) ** block_levels(streams_of[9], (RAYS,), ((0, 8),), -0.2, 0.2), 0.0, 1.0),
        "drop_label": touch_ends((jax.random.randint(streams_of[10], (RAYS,), 0, 4) < 1).astype(jnp.int32), jax.random.fold_in(streams_of[10], 1), 0, 1),
    }


HIGHEST = lax.Precision.HIGHEST
CUBE_OFFSETS = [(a, b, c) for a in range(3) for b in range(3) for c in range(3)]

def unfold_cells(block_set):
    brick_count = block_set.shape[0]
    channel_width = block_set.shape[1]
    cube = block_set.reshape(brick_count, channel_width, 8, 8, 8)
    padded = jnp.pad(cube, ((0, 0), (0, 0), (1, 1), (1, 1), (1, 1)))
    columns = [padded[:, :, a:a + 8, b:b + 8, c:c + 8].reshape(brick_count, channel_width, 512) for a, b, c in CUBE_OFFSETS]
    return jnp.stack(columns, axis=1).reshape(brick_count, 27 * channel_width, 512)

def decode_exact(block_set, weight_full, bias_conv):
    pre_act = jnp.einsum('oc,bcn->bon', weight_full, unfold_cells(block_set), precision=HIGHEST) + bias_conv[None, :, None]
    return jax.nn.gelu(pre_act)

def conv_backward(block_set, block_cot, conv_w, conv_b):
    unfolded = unfold_cells(block_set)
    pre_act = jnp.einsum('oc,bcn->bon', conv_w, unfolded, preferred_element_type=jnp.float32) + conv_b[None, :, None]
    _, gelu_pull = jax.vjp(jax.nn.gelu, pre_act)
    pre_grad = gelu_pull(block_cot)[0].astype(jnp.bfloat16)
    weight_grad = jnp.einsum('bon,bcn->oc', pre_grad, unfolded, preferred_element_type=jnp.float32)
    bias_grad = lax.optimization_barrier(jnp.sum(pre_grad.astype(jnp.float32), axis=(0, 2)))
    column_grad = jnp.einsum('oc,bon->bcn', conv_w, pre_grad, preferred_element_type=jnp.float32)
    _, fold_pull = jax.vjp(unfold_cells, jnp.zeros(block_set.shape, jnp.float32))
    block_grad = fold_pull(column_grad)[0]
    return (weight_grad, bias_grad, block_grad.astype(jnp.bfloat16))

def field_head(feature_cols, weight_one, bias_one, weight_two):
    hidden = jnp.einsum('ch,cm->hm', weight_one, feature_cols, precision=HIGHEST) + bias_one[:, None]
    outputs = jnp.einsum('hk,hm->km', weight_two, jax.nn.gelu(hidden), precision=HIGHEST)
    return (jax.nn.softplus(outputs[0]), jax.nn.sigmoid(outputs[1]))

def render_terms(density, intensity, depth_grid, step_size):
    optical = density * step_size
    before = jnp.cumsum(optical, axis=-1) - optical
    weights = jnp.exp(-before) * (1.0 - jnp.exp(-optical))
    return (lax.optimization_barrier(jnp.sum(weights * depth_grid, axis=-1)), lax.optimization_barrier(jnp.sum(weights * intensity, axis=-1)), lax.optimization_barrier(jnp.sum(optical, axis=-1)))

def reference(bricks, conv_w, conv_b, head_w1, head_b1, head_w2, queries, sample_src, depth_target, inten_target, drop_label):
    weight_full = conv_w.astype(jnp.float32)
    weight_one = head_w1.astype(jnp.float32)
    group_size = math.gcd(BRICK_DEV, 8)
    per_device = RAY_DEV * SAMP
    per_shell = per_device * N_SECTOR

    def decode_shell(shell_bricks):
        groups = shell_bricks.reshape(BRICKS // group_size, group_size, CH, 512)
        result = lax.map(lambda block_set: decode_exact(block_set.astype(jnp.float32), weight_full, conv_b).astype(jnp.bfloat16), groups)
        return result.reshape(BRICKS, CH, 512)
    decoded = lax.map(decode_shell, bricks)

    def locate_cells(shell_id):
        slot_ids = sample_src[shell_id].astype(jnp.int32)
        source_ids = (jnp.arange(per_shell, dtype=jnp.int32) // per_device).astype(jnp.int32)
        owner_ids = slot_ids // CAP
        position = slot_ids % CAP
        address = queries[shell_id][source_ids * N_SECTOR + owner_ids, position]
        return (owner_ids * BRICK_DEV + address // 512, address % 512)

    def sample_features(shell_id):
        brick_ids, cell_ids = locate_cells(shell_id)
        return decoded[shell_id][brick_ids, :, cell_ids].T.astype(jnp.float32)

    def shell_forward(shell_id):
        return field_head(sample_features(shell_id), weight_one, head_b1, head_w2)
    density, intensity = lax.map(shell_forward, jnp.arange(N_SHELL, dtype=jnp.int32))
    density = density.reshape(N_SHELL, RAYS, SAMP)
    intensity = intensity.reshape(N_SHELL, RAYS, SAMP)

    def render_loss(dens_all, inten_all):
        step_size = 2.0 / (N_SHELL * SAMP)
        depth_grid = ((jnp.arange(N_SHELL * SAMP, dtype=jnp.float32).reshape(N_SHELL, SAMP) + 0.5) / (N_SHELL * SAMP))[:, None, :]
        shell_depth, shell_inten, shell_tau = render_terms(dens_all, inten_all, depth_grid, step_size)
        prefix = jnp.cumsum(shell_tau, axis=0) - shell_tau
        entry_trans = jnp.exp(-prefix)
        ray_depth = lax.optimization_barrier(jnp.sum(entry_trans * shell_depth, axis=0))
        ray_inten = lax.optimization_barrier(jnp.sum(entry_trans * shell_inten, axis=0))
        escape = jnp.exp(-lax.optimization_barrier(jnp.sum(shell_tau, axis=0)))
        dropped = drop_label.astype(jnp.float32)
        kept_weight = 1.0 - dropped
        loss_total = jnp.sum(kept_weight * ((ray_depth - depth_target) ** 2 + (ray_inten - inten_target) ** 2) + (escape - dropped) ** 2)
        return (loss_total, ray_depth)
    loss_total, render_pull, ray_depth = jax.vjp(render_loss, density, intensity, has_aux=True)
    dens_grad, inten_grad = render_pull(jnp.ones((), jnp.float32))

    def conv_back(totals, pair_in):
        block_set, block_cot = pair_in
        weight_grad, bias_grad, block_grad = conv_backward(block_set, block_cot, conv_w, conv_b)
        return ((totals[0] + weight_grad, totals[1] + bias_grad), block_grad)

    def shell_backward(carry, shell_id):
        _, head_pull = jax.vjp(field_head, sample_features(shell_id), weight_one, head_b1, head_w2)
        feature_grad, grad_one, grad_bias_one, grad_two = head_pull((dens_grad[shell_id].reshape(-1), inten_grad[shell_id].reshape(-1)))
        brick_ids, cell_ids = locate_cells(shell_id)
        cell_grad = jnp.zeros((BRICKS, CH, 512), jnp.float32).at[brick_ids, :, cell_ids].add(feature_grad.T)
        start = (jnp.zeros_like(weight_full), jnp.zeros_like(conv_b))
        groups = bricks[shell_id].reshape(BRICKS // group_size, group_size, CH, 512)
        cotangents = cell_grad.reshape(BRICKS // group_size, group_size, CH, 512)
        (weight_grad, bias_grad), brick_grads = lax.scan(conv_back, start, (groups, cotangents))
        carry = (carry[0] + weight_grad, carry[1] + bias_grad, carry[2] + grad_one, carry[3] + grad_bias_one, carry[4] + grad_two)
        return (carry, brick_grads.reshape(BRICKS, CH, 512))
    initial = (jnp.zeros_like(weight_full), jnp.zeros_like(conv_b), jnp.zeros_like(weight_one), jnp.zeros_like(head_b1), jnp.zeros_like(head_w2))
    grads, grad_bricks = lax.scan(shell_backward, initial, jnp.arange(N_SHELL, dtype=jnp.int32))
    return (loss_total / RAYS, grads[0], grads[1], grads[2], grads[3], grads[4], grad_bricks, ray_depth)
```

```python
import functools
import math

import jax
import jax.numpy as jnp
from jax import lax
from jax.experimental import pallas as pl
from jax.experimental.pallas import tpu as pltpu
from jax.sharding import PartitionSpec as P

SAMP = 8
MESH = pl.DeviceIdType.MESH
F32 = jnp.float32
BF16 = jnp.bfloat16
GELU_SCALE = math.sqrt(2.0 / math.pi)
GELU_CUBIC = 0.044715
NT = (((1,), (1,)), ((), ()))


def gelu_and_slope(x):
    square = x * x
    t = jnp.tanh(GELU_SCALE * (x + GELU_CUBIC * (x * square)))
    half = 0.5 * (1.0 + t)
    slope = half + 0.5 * x * (1.0 - t * t) * (GELU_SCALE * (1.0 + 3.0 * GELU_CUBIC * square))
    return x * half, slope


def split(value, count):
    pieces = []
    for _ in range(count - 1):
        piece = value.astype(BF16).astype(F32)
        pieces.append(piece)
        value = value - piece
    return pieces + [value]


def matmul(a, b):
    return jnp.dot(a, b, preferred_element_type=F32)


def matmul_nt(a, b):
    return lax.dot_general(a, b, NT, preferred_element_type=F32)


def shifted(x, step, coord):
    width = x.shape[1]
    out = []
    for move in (-1, 0, 1):
        if move == 0:
            out.append(x)
        else:
            rolled = pltpu.roll(x, (-move * step) % width, 1)
            inside = coord >= 1 if move < 0 else coord <= 6
            out.append(rolled * jnp.where(inside, 1.0, 0.0))
    return out


def unfold(x, put):
    lane = lax.broadcasted_iota(jnp.int32, (1, x.shape[1]), 1)
    by_c = shifted(x, 1, lane & 7)
    for c in range(3):
        by_b = shifted(by_c[c], 8, (lane >> 3) & 7)
        for b in range(3):
            by_a = shifted(by_b[b], 64, lane >> 6)
            for a in range(3):
                put(9 * a + 3 * b + c, by_a[a].astype(BF16))


def body(
    shells,
    sectors,
    bricks,
    conv_w,
    conv_back_w,
    conv_b,
    w1_t,
    w1_rep,
    b1,
    w2,
    queries,
    sources,
    depth_target,
    inten_target,
    drop_label,
    grad_bricks,
    ray_depth_out,
    reduced,
    addr,
    decoded,
    slope_conv,
    cols,
    addr_hot,
    src_hot,
    rep_send,
    rep_recv,
    hid_val,
    hid_slope,
    dens_slot,
    inten_slot,
    gd_slot,
    gi_slot,
    shell_buf,
    grad_send,
    grad_recv,
    cell_grad,
    pack,
    red_recv,
    wgrad,
    w1_acc,
    small_acc,
    req_sems,
    rep_sems,
    shell_sems,
    grad_sems,
    red_sems,
    out_sems,
    own_sem,
):
    n = sectors
    count = shells * sectors
    nb, ch, cells = bricks.shape
    cap = queries.shape[2]
    hid = w1_t.shape[0]
    rays = sources.shape[2]
    shift = cap.bit_length() - 1
    shell = lax.axis_index("shell")
    sector = lax.axis_index("sector")
    me = shell * n + sector

    def flat_peer(k):
        peer = lax.rem(me + k, count)
        return peer, {"shell": lax.div(peer, n), "sector": lax.rem(peer, n)}

    barrier = pltpu.get_barrier_semaphore()

    @pl.loop(1, count)
    def _(k):
        _, where = flat_peer(k)
        pl.semaphore_signal(barrier, inc=1, device_id=where, device_id_type=MESH)

    pl.semaphore_wait(barrier, count - 1)

    def to_sector(src, dst, sems, k):
        peer = lax.rem(sector + k, n)
        return pltpu.make_async_remote_copy(
            src_ref=src.at[peer],
            dst_ref=dst.at[sector],
            send_sem=sems.at[0, k],
            recv_sem=sems.at[1, k],
            device_id={"shell": shell, "sector": peer},
            device_id_type=MESH,
        )

    @pl.loop(1, n)
    def _(k):
        to_sector(queries, addr, req_sems, k).start()

    own = pltpu.make_async_copy(queries.at[sector], addr.at[sector], own_sem)
    own.start()

    @pl.loop(0, nb)
    def _(b):
        def put(k, value):
            cols[pl.ds(k * ch, ch), :] = value

        unfold(bricks[b].astype(F32), put)
        pre = matmul(conv_w[...], cols[...]) + conv_b[...]
        value, slope = gelu_and_slope(pre)
        decoded[pl.ds(pl.multiple_of(b * ch, ch), ch), :] = value.astype(BF16)
        slope_conv[pl.ds(pl.multiple_of(b * ch, ch), ch), :] = slope

    own.wait()

    @pl.loop(1, n)
    def _(k):
        to_sector(queries, addr, req_sems, k).wait()

    def gather_for(v, out_ref):
        where = addr[v]
        cell = where & (cells - 1)
        brick = jnp.broadcast_to(where >> (cells.bit_length() - 1), (ch, cap))
        rows = lax.broadcasted_iota(jnp.int32, (cells, cap), 0)
        addr_hot[v] = jnp.where(rows == cell, 1.0, 0.0).astype(BF16)
        picked = matmul(decoded[...], addr_hot[v])
        feats = jnp.zeros((ch, cap), F32)
        for b in range(nb):
            feats = feats + jnp.where(brick == b, picked[b * ch : (b + 1) * ch], 0.0)
        out_ref[v] = feats.astype(BF16)

    @pl.loop(1, n)
    def _(k):
        gather_for(lax.rem(sector + k, n), rep_send)
        to_sector(rep_send, rep_recv, rep_sems, k).start()

    gather_for(sector, rep_recv)

    @pl.loop(0, SAMP)
    def _(k):
        rows = lax.broadcasted_iota(jnp.int32, (cap, rays), 0)
        src_hot[k] = jnp.where(rows == (sources[k] & (cap - 1)), 1.0, 0.0).astype(BF16)

    def head_for(w):
        feats = rep_recv[w]
        value, slope = gelu_and_slope(matmul(w1_t[...], feats) + b1[...])
        hid_val[w] = value
        hid_slope[w] = slope
        dens_slot[pl.ds(w, 1), :] = jnp.sum(value * w2[:, 0:1], axis=0, keepdims=True)
        inten_slot[pl.ds(w, 1), :] = jnp.sum(value * w2[:, 1:2], axis=0, keepdims=True)

    head_for(sector)

    @pl.loop(1, n)
    def _(k):
        to_sector(rep_send, rep_recv, rep_sems, k).wait()
        head_for(lax.rem(sector + n - k, n))

    e0 = dens_slot[...]
    e1 = inten_slot[...]
    dens_all = jnp.maximum(e0, 0.0) + jnp.log1p(jnp.exp(-jnp.abs(e0)))
    inten_all = 1.0 / (1.0 + jnp.exp(-e1))
    slots = jnp.concatenate([dens_all, inten_all], axis=0)
    slot_pieces = jnp.concatenate([p.astype(BF16) for p in split(slots, 3)], axis=0)
    owner_rows = lax.broadcasted_iota(jnp.int32, (n, rays), 0)
    dens = []
    inten = []
    for k in range(SAMP):
        got = matmul(slot_pieces, src_hot[k])
        got = got[: 2 * n] + got[2 * n : 4 * n] + got[4 * n :]
        mine = owner_rows == (sources[k] >> shift)
        dens.append(jnp.sum(jnp.where(mine, got[:n], 0.0), axis=0, keepdims=True))
        inten.append(jnp.sum(jnp.where(mine, got[n:], 0.0), axis=0, keepdims=True))

    step_size = 2.0 / (shells * SAMP)
    span = 1.0 / (shells * SAMP)
    first = shell.astype(F32) * SAMP + 0.5
    before = jnp.zeros((1, rays), F32)
    depth = jnp.zeros((1, rays), F32)
    light = jnp.zeros((1, rays), F32)
    enter = []
    leave = []
    weight = []
    for k in range(SAMP):
        optical = dens[k] * step_size
        enter.append(jnp.exp(-before))
        leave.append(jnp.exp(-optical))
        weight.append(enter[k] * (1.0 - leave[k]))
        depth = depth + weight[k] * ((first + k) * span)
        light = light + weight[k] * inten[k]
        before = before + optical
    shell_buf[shell] = jnp.concatenate(
        [depth, light, before, jnp.zeros((5, rays), F32)], axis=0
    )

    def to_shell(k):
        return pltpu.make_async_remote_copy(
            src_ref=shell_buf.at[shell],
            dst_ref=shell_buf.at[shell],
            send_sem=shell_sems.at[0, k],
            recv_sem=shell_sems.at[1, k],
            device_id={"shell": lax.rem(shell + k, shells), "sector": sector},
            device_id_type=MESH,
        )

    for k in range(1, shells):
        to_shell(k).start()
    for k in range(1, shells):
        to_shell(k).wait()

    prefix = jnp.zeros((1, rays), F32)
    ray_depth = jnp.zeros((1, rays), F32)
    ray_light = jnp.zeros((1, rays), F32)
    entry = []
    for s in range(shells):
        entry.append(jnp.exp(-prefix))
        ray_depth = ray_depth + entry[s] * shell_buf[s, 0:1, :]
        ray_light = ray_light + entry[s] * shell_buf[s, 1:2, :]
        prefix = prefix + shell_buf[s, 2:3, :]
    ray_depth_out[...] = ray_depth
    escape = jnp.exp(-prefix)
    dropped = drop_label[...].astype(F32)
    kept = 1.0 - dropped
    off_depth = ray_depth - depth_target[...]
    off_light = ray_light - inten_target[...]
    off_escape = escape - dropped
    loss = jnp.sum(
        kept * (off_depth * off_depth + off_light * off_light) + off_escape * off_escape,
        axis=1,
        keepdims=True,
    )
    grad_depth = 2.0 * kept * off_depth
    grad_light = 2.0 * kept * off_light
    behind = jnp.zeros((1, rays), F32)
    own_entry = jnp.zeros((1, rays), F32)
    for s in range(shells):
        term = (grad_depth * shell_buf[s, 0:1, :] + grad_light * shell_buf[s, 1:2, :]) * entry[s]
        behind = behind + jnp.where(shell < s, term, 0.0)
        own_entry = own_entry + jnp.where(shell == s, entry[s], 0.0)
    cot_depth = grad_depth * own_entry
    cot_light = grad_light * own_entry
    cot_tau = -2.0 * off_escape * escape - behind
    later = jnp.zeros((1, rays), F32)
    dens_grad = [None] * SAMP
    inten_grad = [None] * SAMP
    for k in reversed(range(SAMP)):
        pull = cot_depth * ((first + k) * span) + cot_light * inten[k]
        inten_grad[k] = cot_light * weight[k]
        dens_grad[k] = step_size * (pull * enter[k] * leave[k] - later + cot_tau)
        later = later + pull * weight[k]
    slot_grad = jnp.zeros((6 * n, cap), F32)
    for k in range(SAMP):
        mine = owner_rows == (sources[k] >> shift)
        both = jnp.concatenate(
            [jnp.where(mine, dens_grad[k], 0.0), jnp.where(mine, inten_grad[k], 0.0)], axis=0
        )
        both = jnp.concatenate([p.astype(BF16) for p in split(both, 3)], axis=0)
        slot_grad = slot_grad + matmul_nt(both, src_hot[k])
    slot_grad = slot_grad[: 2 * n] + slot_grad[2 * n : 4 * n] + slot_grad[4 * n :]
    gd_slot[...] = slot_grad[:n] * (1.0 / (1.0 + jnp.exp(-e0)))
    gi_slot[...] = slot_grad[n:] * (inten_all * (1.0 - inten_all))

    w1_acc[...] = jnp.zeros_like(w1_acc)
    small_acc[...] = jnp.zeros_like(small_acc)

    def head_back(w, out_ref, at):
        g0 = gd_slot[pl.ds(w, 1), :]
        g1 = gi_slot[pl.ds(w, 1), :]
        value = hid_val[w]
        grad = (w2[:, 0:1] * g0 + w2[:, 1:2] * g1) * hid_slope[w]
        pieces = jnp.concatenate([p.astype(BF16) for p in split(grad, 3)], axis=0)
        out_ref[at] = matmul(w1_rep[...], pieces)
        w1_acc[...] += matmul_nt(rep_recv[w], pieces)
        small_acc[0] += jnp.sum(grad, axis=1, keepdims=True)
        small_acc[1] += jnp.sum(value * g0, axis=1, keepdims=True)
        small_acc[2] += jnp.sum(value * g1, axis=1, keepdims=True)

    @pl.loop(1, n)
    def _(k):
        w = lax.rem(sector + k, n)
        head_back(w, grad_send, w)
        to_sector(grad_send, grad_recv, grad_sems, k).start()

    head_back(sector, grad_recv, sector)

    cell_grad[...] = jnp.zeros_like(cell_grad)

    def scatter_from(v):
        brick = jnp.broadcast_to(addr[v] >> (cells.bit_length() - 1), (ch, cap))
        high, low = split(grad_recv[v], 2)
        spread = jnp.concatenate(
            [jnp.where(brick == b, p, 0.0).astype(BF16) for p in (high, low) for b in range(nb)],
            axis=0,
        )
        added = matmul_nt(spread, addr_hot[v])
        cell_grad[...] += added[: nb * ch] + added[nb * ch :]

    scatter_from(sector)

    @pl.loop(1, n)
    def _(k):
        to_sector(grad_send, grad_recv, grad_sems, k).wait()
        scatter_from(lax.rem(sector + n - k, n))

    wgrad[...] = jnp.zeros_like(wgrad)
    wide = wgrad.shape[1]
    used = 27 * ch

    def conv_back(b, bias):
        def put(k, value):
            cols[pl.ds(k * ch, ch), :] = value

        at = pl.ds(pl.multiple_of(b * ch, ch), ch)
        cot = (cell_grad[at, :] * slope_conv[at, :]).astype(BF16)
        unfold(cot.astype(F32), put)
        grad_bricks[b] = matmul(conv_back_w[...], cols[...]).astype(BF16)
        wgrad[:, :used] += matmul_nt(bricks[b], cols[...])
        return bias + jnp.sum(cot.astype(F32), axis=1, keepdims=True)

    bias_grad = lax.fori_loop(0, nb, conv_back, jnp.zeros((ch, 1), F32))

    tiles = wide // 128
    for t in range(tiles):
        for part in range(ch // 8):
            pack[t * (ch // 8) + part] = wgrad[part * 8 : part * 8 + 8, t * 128 : t * 128 + 128]
    lane = lax.broadcasted_iota(jnp.int32, (ch, 128), 1)
    w1_all = w1_acc[...]
    w1_grad = w1_all[:, :hid] + w1_all[:, hid : 2 * hid] + w1_all[:, 2 * hid :]
    last = jnp.concatenate([w1_grad, jnp.zeros((ch, 128 - hid), F32)], axis=1)
    place = hid
    for j in range(3):
        for part in range(hid // ch):
            column = small_acc[j, part * ch : (part + 1) * ch, :]
            last = last + jnp.where(lane == place, column, 0.0)
            place += 1
    last = last + jnp.where(lane == place, bias_grad, 0.0)
    loss_here = jnp.where(shell == 0, loss, 0.0)
    last = last + jnp.where(lane == place + 1, loss_here, 0.0)
    base = tiles * (ch // 8)
    for part in range(ch // 8):
        pack[base + part] = last[part * 8 : part * 8 + 8]
    for extra in range(base + ch // 8, pack.shape[0]):
        pack[extra] = jnp.zeros((8, 128), F32)

    def to_reducer(k):
        peer, where = flat_peer(k)
        return pltpu.make_async_remote_copy(
            src_ref=pack.at[peer],
            dst_ref=red_recv.at[me],
            send_sem=red_sems.at[0, k],
            recv_sem=red_sems.at[1, k],
            device_id=where,
            device_id_type=MESH,
        )

    def to_everyone(k):
        _, where = flat_peer(k)
        return pltpu.make_async_remote_copy(
            src_ref=reduced.at[me],
            dst_ref=reduced.at[me],
            send_sem=out_sems.at[0, k],
            recv_sem=out_sems.at[1, k],
            device_id=where,
            device_id_type=MESH,
        )

    @pl.loop(1, count)
    def _(k):
        to_reducer(k).start()

    red_recv[me] = pack[me]

    @pl.loop(1, count)
    def _(k):
        to_reducer(k).wait()

    reduced[me] = jnp.sum(red_recv[...], axis=0)

    @pl.loop(1, count)
    def _(k):
        to_everyone(k).start()

    @pl.loop(1, count)
    def _(k):
        to_everyone(k).wait()


def local(
    bricks,
    conv_w,
    conv_b,
    head_w1,
    head_b1,
    head_w2,
    queries,
    sample_src,
    depth_target,
    inten_target,
    drop_label,
):
    shells = lax.axis_size("shell")
    n = lax.axis_size("sector")
    count = shells * n
    _, nb, ch, cells = bricks.shape
    cap = queries.shape[2]
    hid = head_w1.shape[1]
    rays = depth_target.shape[0]
    wide = -(-27 * ch // 128) * 128
    chunks = (wide // 128 + 1) * (ch // 8)
    held = max(count, -(-chunks // count) * count)
    assert held == count and cap & (cap - 1) == 0 and cells == 512
    conv_back_w = conv_w.reshape(ch, 27, ch)[:, ::-1].transpose(2, 1, 0).reshape(ch, 27 * ch)
    operands = (
        bricks[0],
        conv_w,
        conv_back_w,
        conv_b[:, None],
        head_w1.T,
        jnp.concatenate([head_w1] * 3, axis=1),
        head_b1[:, None],
        head_w2,
        queries[0][:, None, :],
        sample_src[0].reshape(rays, SAMP).T[:, None, :],
        depth_target[None],
        inten_target[None],
        drop_label[None],
    )
    vmem = pl.BlockSpec(memory_space=pltpu.VMEM)
    dma = pltpu.SemaphoreType.DMA
    grad_bricks, ray_depth, reduced = pl.pallas_call(
        functools.partial(body, shells, n),
        out_shape=(
            jax.ShapeDtypeStruct((nb, ch, cells), BF16),
            jax.ShapeDtypeStruct((1, rays), F32),
            jax.ShapeDtypeStruct((held, 8, 128), F32),
        ),
        in_specs=[vmem] * len(operands),
        out_specs=(vmem, vmem, vmem),
        scratch_shapes=[
            pltpu.VMEM((n, 1, cap), jnp.int32),
            pltpu.VMEM((nb * ch, cells), BF16),
            pltpu.VMEM((nb * ch, cells), F32),
            pltpu.VMEM((27 * ch, cells), BF16),
            pltpu.VMEM((n, cells, cap), BF16),
            pltpu.VMEM((SAMP, cap, rays), BF16),
            pltpu.VMEM((n, ch, cap), BF16),
            pltpu.VMEM((n, ch, cap), BF16),
            pltpu.VMEM((n, hid, cap), F32),
            pltpu.VMEM((n, hid, cap), F32),
            pltpu.VMEM((n, cap), F32),
            pltpu.VMEM((n, cap), F32),
            pltpu.VMEM((n, cap), F32),
            pltpu.VMEM((n, cap), F32),
            pltpu.VMEM((shells, 8, rays), F32),
            pltpu.VMEM((n, ch, cap), F32),
            pltpu.VMEM((n, ch, cap), F32),
            pltpu.VMEM((nb * ch, cells), F32),
            pltpu.VMEM((held, 8, 128), F32),
            pltpu.VMEM((count, 8, 128), F32),
            pltpu.VMEM((ch, wide), F32),
            pltpu.VMEM((ch, 3 * hid), F32),
            pltpu.VMEM((3, hid, 1), F32),
            dma((2, n)),
            dma((2, n)),
            dma((2, shells)),
            dma((2, n)),
            dma((2, count)),
            dma((2, count)),
            dma,
        ],
        compiler_params=pltpu.CompilerParams(
            collective_id=0, has_side_effects=True, vmem_limit_bytes=56 * 1024 * 1024
        ),
    )(*operands)
    tiles = wide // 128
    flat = reduced.reshape(-1, 128)
    conv_grad = flat[: tiles * ch].reshape(tiles, ch, 128).transpose(1, 0, 2).reshape(ch, wide)
    conv_grad = conv_grad[:, : 27 * ch].reshape(ch, 27, ch)[:, ::-1].transpose(2, 1, 0)
    last = flat[tiles * ch : (tiles + 1) * ch]
    per = hid // ch
    columns = last[:, hid : hid + 3 * per].T.reshape(3, hid)
    place = hid + 3 * per
    return (
        last[0, place + 1] / (rays * n),
        conv_grad.reshape(ch, 27 * ch),
        last[:, place],
        last[:, :hid],
        columns[0],
        columns[1:].T,
        grad_bricks[None],
        ray_depth[0],
    )


def solution(mesh):
    return jax.shard_map(
        local,
        mesh=mesh,
        in_specs=(
            P("shell", "sector", None, None),
            P(),
            P(),
            P(),
            P(),
            P(),
            P("shell", "sector", None),
            P("shell", "sector"),
            P("sector"),
            P("sector"),
            P("sector"),
        ),
        out_specs=(P(), P(), P(), P(), P(), P(), P("shell", "sector", None, None), P("sector")),
        check_vma=False,
    )
```

```python
import functools
import math

import jax
import jax.numpy as jnp
from jax import lax
from jax.experimental import pallas as pl
from jax.experimental.pallas import tpu as pltpu
from jax.sharding import PartitionSpec as P

SAMP = 8
MESH = pl.DeviceIdType.MESH
F32 = jnp.float32
BF16 = jnp.bfloat16
GELU_SCALE = math.sqrt(2.0 / math.pi)
GELU_CUBIC = 0.044715
NT = (((1,), (1,)), ((), ()))


def gelu_and_slope(x):
    square = x * x
    t = jnp.tanh(GELU_SCALE * (x + GELU_CUBIC * (x * square)))
    half = 0.5 * (1.0 + t)
    slope = half + 0.5 * x * (1.0 - t * t) * (GELU_SCALE * (1.0 + 3.0 * GELU_CUBIC * square))
    return x * half, slope


def split(value, count):
    pieces = []
    for _ in range(count - 1):
        piece = value.astype(BF16).astype(F32)
        pieces.append(piece)
        value = value - piece
    return pieces + [value]


def matmul(a, b):
    return jnp.dot(a, b, preferred_element_type=F32)


def matmul_nt(a, b):
    return lax.dot_general(a, b, NT, preferred_element_type=F32)


def shifted(x, step, coord):
    width = x.shape[1]
    out = []
    for move in (-1, 0, 1):
        if move == 0:
            out.append(x)
        else:
            rolled = pltpu.roll(x, (-move * step) % width, 1)
            inside = coord >= 1 if move < 0 else coord <= 6
            out.append(rolled * jnp.where(inside, 1.0, 0.0))
    return out


def unfold(x, put):
    lane = lax.broadcasted_iota(jnp.int32, (1, x.shape[1]), 1)
    by_c = shifted(x, 1, lane & 7)
    for c in range(3):
        by_b = shifted(by_c[c], 8, (lane >> 3) & 7)
        for b in range(3):
            by_a = shifted(by_b[b], 64, lane >> 6)
            for a in range(3):
                put(9 * a + 3 * b + c, by_a[a].astype(BF16))


def column(row):
    size = row.shape[1]
    i = lax.broadcasted_iota(jnp.int32, (size, size), 0)
    j = lax.broadcasted_iota(jnp.int32, (size, size), 1)
    return jnp.sum(jnp.where(i == j, row, 0.0), axis=1, keepdims=True)


def repeated_eye(size, times):
    i = lax.broadcasted_iota(jnp.int32, (size, size), 0)
    j = lax.broadcasted_iota(jnp.int32, (size, size), 1)
    eye = jnp.where(i == j, 1.0, 0.0)
    return jnp.concatenate([eye] * times, axis=1).astype(BF16)


def body(
    shells,
    sectors,
    bricks,
    conv_w,
    conv_b,
    w1,
    b1,
    w2,
    queries,
    sample_src,
    depth_target,
    inten_target,
    drop_label,
    grad_bricks,
    ray_depth_out,
    reduced,
    conv_back_w,
    w1_t,
    w1_rep,
    sources,
    asked,
    addr,
    decoded,
    slope_conv,
    cols,
    cot_cols,
    addr_hot,
    src_hot,
    rep_send,
    rep_recv,
    hid_val,
    hid_slope,
    dens_slot,
    inten_slot,
    gd_slot,
    gi_slot,
    shell_buf,
    grad_send,
    grad_recv,
    cell_grad,
    pack,
    red_recv,
    req_sems,
    rep_sems,
    shell_sems,
    grad_sems,
    red_sems,
    out_sems,
    own_sem,
):
    n = sectors
    count = shells * sectors
    nb, ch, cells = bricks.shape
    cap = queries.shape[1]
    hid = w1.shape[1]
    rays = sources.shape[1]
    shift = cap.bit_length() - 1
    shell = lax.axis_index("shell")
    sector = lax.axis_index("sector")
    me = shell * n + sector

    def flat_peer(k):
        peer = lax.rem(me + k, count)
        return peer, {"shell": lax.div(peer, n), "sector": lax.rem(peer, n)}

    barrier = pltpu.get_barrier_semaphore()

    @pl.loop(1, count)
    def _(k):
        _, where = flat_peer(k)
        pl.semaphore_signal(barrier, inc=1, device_id=where, device_id_type=MESH)

    for j in range(n):
        asked[j] = queries[j : j + 1, :]
    conv_b_col = column(conv_b[...])
    b1_col = column(b1[...])
    w2_density = column(w2[0:1, :])
    w2_intensity = column(w2[1:2, :])
    w1_t[...] = matmul_nt(repeated_eye(hid, 1), w1[...]).astype(BF16)
    w1_rep[...] = matmul(w1[...], repeated_eye(hid, 3)).astype(BF16)
    turned = jnp.transpose(conv_w[...].astype(F32))
    conv_back_w[...] = jnp.concatenate(
        [turned[k * ch : (k + 1) * ch] for k in reversed(range(27))], axis=1
    ).astype(BF16)
    block = SAMP * 128
    ray_of = lax.broadcasted_iota(jnp.int32, (block, 128), 0) // SAMP
    to_ray = jnp.where(ray_of == lax.broadcasted_iota(jnp.int32, (block, 128), 1), 1.0, 0.0)
    to_ray = to_ray.astype(BF16)
    sample_of = lax.broadcasted_iota(jnp.int32, (SAMP, block), 1) & (SAMP - 1)
    own_row = sample_of == lax.broadcasted_iota(jnp.int32, (SAMP, block), 0)
    for j in range(rays // 128):
        part = sample_src[:, j * block : (j + 1) * block]
        pair = [(part >> 7).astype(F32), (part & 127).astype(F32)]
        pair = jnp.concatenate([jnp.where(own_row, p, 0.0) for p in pair], axis=0)
        got = matmul(pair.astype(BF16), to_ray)
        whole = got[:SAMP] * 128.0 + got[SAMP:]
        sources[:, j * 128 : (j + 1) * 128] = whole.astype(jnp.int32)

    pl.semaphore_wait(barrier, count - 1)

    def to_owner(src, dst, sems, k):
        return pltpu.make_async_remote_copy(
            src_ref=src,
            dst_ref=dst.at[k],
            send_sem=sems.at[0, k],
            recv_sem=sems.at[1, k],
            device_id={"shell": shell, "sector": lax.rem(sector + k, n)},
            device_id_type=MESH,
        )

    def to_asker(src, dst, sems, k):
        return pltpu.make_async_remote_copy(
            src_ref=src,
            dst_ref=dst.at[k],
            send_sem=sems.at[0, k],
            recv_sem=sems.at[1, k],
            device_id={"shell": shell, "sector": lax.rem(sector + n - k, n)},
            device_id_type=MESH,
        )

    def request(k):
        return to_owner(asked.at[lax.rem(sector + k, n)], addr, req_sems, k)

    def reply(k):
        return to_asker(rep_send.at[k], rep_recv, rep_sems, k)

    def give_back(k):
        return to_owner(grad_send.at[k], grad_recv, grad_sems, k)

    for k in range(1, n):
        request(k).start()

    own = pltpu.make_async_copy(asked.at[sector], addr.at[0], own_sem)
    own.start()

    for b in range(nb):

        def put(k, value, b=b):
            cols[b, k * ch : (k + 1) * ch, :] = value

        unfold(bricks[b].astype(F32), put)
        value, slope = gelu_and_slope(matmul(conv_w[...], cols[b]) + conv_b_col)
        decoded[b * ch : (b + 1) * ch, :] = value.astype(BF16)
        slope_conv[b * ch : (b + 1) * ch, :] = slope

    own.wait()
    for k in range(1, n):
        request(k).wait()

    def gather_for(k, out_ref):
        where = addr[k]
        cell = where & (cells - 1)
        brick = jnp.broadcast_to(where >> (cells.bit_length() - 1), (ch, cap))
        rows = lax.broadcasted_iota(jnp.int32, (cells, cap), 0)
        addr_hot[k] = jnp.where(rows == cell, 1.0, 0.0).astype(BF16)
        picked = matmul(decoded[...], addr_hot[k])
        feats = jnp.zeros((ch, cap), F32)
        for b in range(nb):
            feats = feats + jnp.where(brick == b, picked[b * ch : (b + 1) * ch], 0.0)
        out_ref[k] = feats.astype(BF16)

    for k in range(1, n):
        gather_for(k, rep_send)
        reply(k).start()
    gather_for(0, rep_recv)

    for k in range(SAMP):
        rows = lax.broadcasted_iota(jnp.int32, (cap, rays), 0)
        slot = sources[k : k + 1, :] & (cap - 1)
        src_hot[k] = jnp.where(rows == slot, 1.0, 0.0).astype(BF16)

    for k in range(n):
        if k > 0:
            reply(k).wait()
        value, slope = gelu_and_slope(matmul(w1_t[...], rep_recv[k]) + b1_col)
        hid_val[k] = value
        hid_slope[k] = slope
        dens_slot[k : k + 1, :] = jnp.sum(value * w2_density, axis=0, keepdims=True)
        inten_slot[k : k + 1, :] = jnp.sum(value * w2_intensity, axis=0, keepdims=True)

    e0 = dens_slot[...]
    e1 = inten_slot[...]
    dens_all = jnp.maximum(e0, 0.0) + jnp.log1p(jnp.exp(-jnp.abs(e0)))
    inten_all = 1.0 / (1.0 + jnp.exp(-e1))
    slots = jnp.concatenate([dens_all, inten_all], axis=0)
    slot_pieces = jnp.concatenate([p.astype(BF16) for p in split(slots, 3)], axis=0)
    owner_rows = lax.broadcasted_iota(jnp.int32, (n, rays), 0)
    owner_of = (sources[...] >> shift) - sector
    owner_of = jnp.where(owner_of < 0, owner_of + n, owner_of)
    dens = []
    inten = []
    for k in range(SAMP):
        got = matmul(slot_pieces, src_hot[k])
        got = got[: 2 * n] + got[2 * n : 4 * n] + got[4 * n :]
        mine = owner_rows == owner_of[k : k + 1, :]
        dens.append(jnp.sum(jnp.where(mine, got[:n], 0.0), axis=0, keepdims=True))
        inten.append(jnp.sum(jnp.where(mine, got[n:], 0.0), axis=0, keepdims=True))

    step_size = 2.0 / (shells * SAMP)
    span = 1.0 / (shells * SAMP)
    first = shell.astype(F32) * SAMP + 0.5
    before = jnp.zeros((1, rays), F32)
    depth = jnp.zeros((1, rays), F32)
    light = jnp.zeros((1, rays), F32)
    enter = []
    leave = []
    weight = []
    for k in range(SAMP):
        optical = dens[k] * step_size
        enter.append(jnp.exp(-before))
        leave.append(jnp.exp(-optical))
        weight.append(enter[k] * (1.0 - leave[k]))
        depth = depth + weight[k] * ((first + k) * span)
        light = light + weight[k] * inten[k]
        before = before + optical
    shell_buf[shell] = jnp.concatenate(
        [depth, light, before, jnp.zeros((5, rays), F32)], axis=0
    )

    def to_shell(k):
        return pltpu.make_async_remote_copy(
            src_ref=shell_buf.at[shell],
            dst_ref=shell_buf.at[shell],
            send_sem=shell_sems.at[0, k],
            recv_sem=shell_sems.at[1, k],
            device_id={"shell": lax.rem(shell + k, shells), "sector": sector},
            device_id_type=MESH,
        )

    for k in range(1, shells):
        to_shell(k).start()
    for k in range(1, shells):
        to_shell(k).wait()

    prefix = jnp.zeros((1, rays), F32)
    ray_depth = jnp.zeros((1, rays), F32)
    ray_light = jnp.zeros((1, rays), F32)
    entry = []
    for s in range(shells):
        entry.append(jnp.exp(-prefix))
        ray_depth = ray_depth + entry[s] * shell_buf[s, 0:1, :]
        ray_light = ray_light + entry[s] * shell_buf[s, 1:2, :]
        prefix = prefix + shell_buf[s, 2:3, :]
    ray_depth_out[...] = ray_depth
    escape = jnp.exp(-prefix)
    dropped = drop_label[...].astype(F32)
    kept = 1.0 - dropped
    off_depth = ray_depth - depth_target[...]
    off_light = ray_light - inten_target[...]
    off_escape = escape - dropped
    loss = jnp.sum(
        kept * (off_depth * off_depth + off_light * off_light) + off_escape * off_escape,
        axis=1,
        keepdims=True,
    )
    grad_depth = 2.0 * kept * off_depth
    grad_light = 2.0 * kept * off_light
    behind = jnp.zeros((1, rays), F32)
    own_entry = jnp.zeros((1, rays), F32)
    for s in range(shells):
        term = (grad_depth * shell_buf[s, 0:1, :] + grad_light * shell_buf[s, 1:2, :]) * entry[s]
        behind = behind + jnp.where(shell < s, term, 0.0)
        own_entry = own_entry + jnp.where(shell == s, entry[s], 0.0)
    cot_depth = grad_depth * own_entry
    cot_light = grad_light * own_entry
    cot_tau = -2.0 * off_escape * escape - behind
    later = jnp.zeros((1, rays), F32)
    dens_grad = [None] * SAMP
    inten_grad = [None] * SAMP
    for k in reversed(range(SAMP)):
        pull = cot_depth * ((first + k) * span) + cot_light * inten[k]
        inten_grad[k] = cot_light * weight[k]
        dens_grad[k] = step_size * (pull * enter[k] * leave[k] - later + cot_tau)
        later = later + pull * weight[k]
    slot_grad = jnp.zeros((6 * n, cap), F32)
    for k in range(SAMP):
        mine = owner_rows == owner_of[k : k + 1, :]
        both = jnp.concatenate(
            [jnp.where(mine, dens_grad[k], 0.0), jnp.where(mine, inten_grad[k], 0.0)], axis=0
        )
        both = jnp.concatenate([p.astype(BF16) for p in split(both, 3)], axis=0)
        slot_grad = slot_grad + matmul_nt(both, src_hot[k])
    slot_grad = slot_grad[: 2 * n] + slot_grad[2 * n : 4 * n] + slot_grad[4 * n :]
    gd_slot[...] = slot_grad[:n] * (1.0 / (1.0 + jnp.exp(-e0)))
    gi_slot[...] = slot_grad[n:] * (inten_all * (1.0 - inten_all))

    w1_acc = jnp.zeros((ch, 3 * hid), F32)
    small = [jnp.zeros((hid, 1), F32)] * 3
    for k in [*range(1, n), 0]:
        g0 = gd_slot[k : k + 1, :]
        g1 = gi_slot[k : k + 1, :]
        value = hid_val[k]
        grad = (w2_density * g0 + w2_intensity * g1) * hid_slope[k]
        pieces = jnp.concatenate([p.astype(BF16) for p in split(grad, 3)], axis=0)
        if k > 0:
            grad_send[k] = matmul(w1_rep[...], pieces)
            give_back(k).start()
        else:
            grad_recv[k] = matmul(w1_rep[...], pieces)
        w1_acc = w1_acc + matmul_nt(rep_recv[k], pieces)
        terms = (grad, value * g0, value * g1)
        small = [a + jnp.sum(t, axis=1, keepdims=True) for a, t in zip(small, terms)]

    for k in range(n):
        if k > 0:
            give_back(k).wait()
        brick = jnp.broadcast_to(addr[k] >> (cells.bit_length() - 1), (ch, cap))
        high, low = split(grad_recv[k], 2)
        spread = jnp.concatenate(
            [jnp.where(brick == b, p, 0.0).astype(BF16) for p in (high, low) for b in range(nb)],
            axis=0,
        )
        added = matmul_nt(spread, addr_hot[k])
        added = added[: nb * ch] + added[nb * ch :]
        cell_grad[...] = added if k == 0 else cell_grad[...] + added

    used = 27 * ch
    wide = -(-used // 128) * 128
    wgrad = jnp.zeros((ch, used), F32)
    bias_grad = jnp.zeros((ch, 1), F32)
    for b in range(nb):

        def put(k, value, b=b):
            cot_cols[b, k * ch : (k + 1) * ch, :] = value

        at = slice(b * ch, (b + 1) * ch)
        cot = (cell_grad[at, :] * slope_conv[at, :]).astype(BF16)
        unfold(cot.astype(F32), put)
        grad_bricks[b] = matmul(conv_back_w[...], cot_cols[b]).astype(BF16)
        wgrad = wgrad + matmul_nt(cot, cols[b])
        bias_grad = bias_grad + jnp.sum(cot.astype(F32), axis=1, keepdims=True)

    tiles = wide // 128
    wgrad = jnp.concatenate([wgrad, jnp.zeros((ch, wide - used), F32)], axis=1)
    for t in range(tiles):
        for part in range(ch // 8):
            pack[t * (ch // 8) + part] = wgrad[part * 8 : part * 8 + 8, t * 128 : t * 128 + 128]
    lane = lax.broadcasted_iota(jnp.int32, (ch, 128), 1)
    w1_grad = w1_acc[:, :hid] + w1_acc[:, hid : 2 * hid] + w1_acc[:, 2 * hid :]
    last = jnp.concatenate([w1_grad, jnp.zeros((ch, 128 - hid), F32)], axis=1)
    place = hid
    for j in range(3):
        for part in range(hid // ch):
            values = small[j][part * ch : (part + 1) * ch, :]
            last = last + jnp.where(lane == place, values, 0.0)
            place += 1
    last = last + jnp.where(lane == place, bias_grad, 0.0)
    loss_here = jnp.where(shell == 0, loss, 0.0)
    last = last + jnp.where(lane == place + 1, loss_here, 0.0)
    base = tiles * (ch // 8)
    for part in range(ch // 8):
        pack[base + part] = last[part * 8 : part * 8 + 8]
    for extra in range(base + ch // 8, pack.shape[0]):
        pack[extra] = jnp.zeros((8, 128), F32)

    def to_reducer(k):
        peer, where = flat_peer(k)
        return pltpu.make_async_remote_copy(
            src_ref=pack.at[peer],
            dst_ref=red_recv.at[me],
            send_sem=red_sems.at[0, k],
            recv_sem=red_sems.at[1, k],
            device_id=where,
            device_id_type=MESH,
        )

    def to_everyone(k):
        _, where = flat_peer(k)
        return pltpu.make_async_remote_copy(
            src_ref=reduced.at[me],
            dst_ref=reduced.at[me],
            send_sem=out_sems.at[0, k],
            recv_sem=out_sems.at[1, k],
            device_id=where,
            device_id_type=MESH,
        )

    @pl.loop(1, count)
    def _(k):
        to_reducer(k).start()

    red_recv[me] = pack[me]

    @pl.loop(1, count)
    def _(k):
        to_reducer(k).wait()

    reduced[me] = jnp.sum(red_recv[...], axis=0)

    @pl.loop(1, count)
    def _(k):
        to_everyone(k).start()

    @pl.loop(1, count)
    def _(k):
        to_everyone(k).wait()


def finish(
    scale,
    reduced,
    grad_bricks,
    ray_depth,
    loss_out,
    conv_out,
    conv_b_out,
    w1_out,
    b1_out,
    w2_out,
    bricks_out,
    depth_out,
):
    ch, used = conv_out.shape
    hid = w1_out.shape[1]
    per = ch // 8
    tiles = -(-used // 128)
    for t in range(tiles):
        stop = min(128, used - t * 128)
        for part in range(per):
            conv_out[part * 8 : part * 8 + 8, t * 128 : t * 128 + stop] = reduced[
                t * per + part, :, :stop
            ]
    last = jnp.concatenate([reduced[tiles * per + part] for part in range(per)], axis=0)
    w1_out[...] = last[:, :hid]

    def row(place, count):
        i = lax.broadcasted_iota(jnp.int32, (ch, ch * count), 0)
        j = lax.broadcasted_iota(jnp.int32, (ch, ch * count), 1)
        total = jnp.zeros((1, ch * count), F32)
        for part in range(count):
            spread = jnp.where(j == i + part * ch, last[:, place + part : place + part + 1], 0.0)
            total = total + jnp.sum(spread, axis=0, keepdims=True)
        return total

    count = hid // ch
    b1_out[...] = row(hid, count)
    w2_out[0:1, :] = row(hid + count, count)
    w2_out[1:2, :] = row(hid + 2 * count, count)
    place = hid + 3 * count
    conv_b_out[...] = row(place, 1)
    loss_out[...] = last[0:1, place + 1 : place + 2] * scale
    bricks_out[...] = grad_bricks[...]
    depth_out[...] = ray_depth[...]


def local(
    bricks,
    conv_w,
    conv_b,
    head_w1,
    head_b1,
    head_w2,
    queries,
    sample_src,
    depth_target,
    inten_target,
    drop_label,
):
    shells = lax.axis_size("shell")
    n = lax.axis_size("sector")
    count = shells * n
    _, nb, ch, cells = bricks.shape
    cap = queries.shape[2]
    hid = head_w1.shape[1]
    rays = depth_target.shape[0]
    chunks = (-(-27 * ch // 128) + 1) * (ch // 8)
    assert chunks <= count and cap & (cap - 1) == 0 and cells == 512 and rays % 128 == 0
    operands = (
        bricks[0],
        conv_w,
        conv_b[None],
        head_w1,
        head_b1[None],
        head_w2.T,
        queries[0],
        sample_src,
        depth_target[None],
        inten_target[None],
        drop_label[None],
    )
    vmem = pl.BlockSpec(memory_space=pltpu.VMEM)
    dma = pltpu.SemaphoreType.DMA
    grad_bricks, ray_depth, reduced = pl.pallas_call(
        functools.partial(body, shells, n),
        out_shape=(
            jax.ShapeDtypeStruct((nb, ch, cells), BF16),
            jax.ShapeDtypeStruct((1, rays), F32),
            jax.ShapeDtypeStruct((count, 8, 128), F32),
        ),
        in_specs=[vmem] * len(operands),
        out_specs=(vmem, vmem, vmem),
        scratch_shapes=[
            pltpu.VMEM((ch, 27 * ch), BF16),
            pltpu.VMEM((hid, ch), BF16),
            pltpu.VMEM((ch, 3 * hid), BF16),
            pltpu.VMEM((SAMP, rays), jnp.int32),
            pltpu.VMEM((n, 1, cap), jnp.int32),
            pltpu.VMEM((n, 1, cap), jnp.int32),
            pltpu.VMEM((nb * ch, cells), BF16),
            pltpu.VMEM((nb * ch, cells), F32),
            pltpu.VMEM((nb, 27 * ch, cells), BF16),
            pltpu.VMEM((nb, 27 * ch, cells), BF16),
            pltpu.VMEM((n, cells, cap), BF16),
            pltpu.VMEM((SAMP, cap, rays), BF16),
            pltpu.VMEM((n, ch, cap), BF16),
            pltpu.VMEM((n, ch, cap), BF16),
            pltpu.VMEM((n, hid, cap), F32),
            pltpu.VMEM((n, hid, cap), F32),
            pltpu.VMEM((n, cap), F32),
            pltpu.VMEM((n, cap), F32),
            pltpu.VMEM((n, cap), F32),
            pltpu.VMEM((n, cap), F32),
            pltpu.VMEM((shells, 8, rays), F32),
            pltpu.VMEM((n, ch, cap), F32),
            pltpu.VMEM((n, ch, cap), F32),
            pltpu.VMEM((nb * ch, cells), F32),
            pltpu.VMEM((count, 8, 128), F32),
            pltpu.VMEM((count, 8, 128), F32),
            dma((2, n)),
            dma((2, n)),
            dma((2, shells)),
            dma((2, n)),
            dma((2, count)),
            dma((2, count)),
            dma,
        ],
        compiler_params=pltpu.CompilerParams(
            collective_id=0, has_side_effects=True, vmem_limit_bytes=56 * 1024 * 1024
        ),
    )(*operands)
    loss, conv_grad, conv_b_grad, w1_grad, b1_grad, w2_grad, grad_bricks, ray_depth = pl.pallas_call(
        functools.partial(finish, 1.0 / (rays * n)),
        out_shape=(
            jax.ShapeDtypeStruct((1, 1), F32),
            jax.ShapeDtypeStruct((ch, 27 * ch), F32),
            jax.ShapeDtypeStruct((1, ch), F32),
            jax.ShapeDtypeStruct((ch, hid), F32),
            jax.ShapeDtypeStruct((1, hid), F32),
            jax.ShapeDtypeStruct((2, hid), F32),
            jax.ShapeDtypeStruct((nb, ch, cells), BF16),
            jax.ShapeDtypeStruct((1, rays), F32),
        ),
        in_specs=[vmem] * 3,
        out_specs=(vmem,) * 8,
    )(reduced, grad_bricks, ray_depth)
    return (
        loss[0, 0],
        conv_grad,
        conv_b_grad[0],
        w1_grad,
        b1_grad[0],
        w2_grad.T,
        grad_bricks[None],
        ray_depth[0],
    )


def solution(mesh):
    return jax.shard_map(
        local,
        mesh=mesh,
        in_specs=(
            P("shell", "sector", None, None),
            P(),
            P(),
            P(),
            P(),
            P(),
            P("shell", "sector", None),
            P("shell", "sector"),
            P("sector"),
            P("sector"),
            P("sector"),
        ),
        out_specs=(P(), P(), P(), P(), P(), P(), P("shell", "sector", None, None), P("sector")),
        check_vma=False,
    )
```

```python
import functools
import math

import jax
import jax.numpy as jnp
from jax import lax
from jax.experimental import pallas as pl
from jax.experimental.pallas import tpu as pltpu
from jax.sharding import PartitionSpec as P

SAMP = 8
MESH = pl.DeviceIdType.MESH
F32 = jnp.float32
BF16 = jnp.bfloat16
GELU_SCALE = math.sqrt(2.0 / math.pi)
GELU_CUBIC = 0.044715
NT = (((1,), (1,)), ((), ()))


def gelu_and_slope(x):
    square = x * x
    t = jnp.tanh(GELU_SCALE * (x + GELU_CUBIC * (x * square)))
    half = 0.5 * (1.0 + t)
    slope = half + 0.5 * x * (1.0 - t * t) * (GELU_SCALE * (1.0 + 3.0 * GELU_CUBIC * square))
    return x * half, slope


def split(value, count):
    pieces = []
    for _ in range(count - 1):
        piece = value.astype(BF16).astype(F32)
        pieces.append(piece)
        value = value - piece
    return pieces + [value]


def matmul(a, b):
    return jnp.dot(a, b, preferred_element_type=F32)


def matmul_nt(a, b):
    return lax.dot_general(a, b, NT, preferred_element_type=F32)


def moved(x, step, coord, move):
    if move == 0:
        return x
    rolled = pltpu.roll(x, (-move * step) % x.shape[1], 1)
    inside = coord >= 1 if move < 0 else coord <= 6
    return rolled * jnp.where(inside, 1.0, 0.0)


def unfold(x, out, lane):
    ch = x.shape[0]
    for c in range(3):
        by_c = moved(x, 1, lane & 7, c - 1)
        for b in range(3):
            k = 3 * b + c
            value = moved(by_c, 8, (lane >> 3) & 7, b - 1)
            out[k * ch : (k + 1) * ch, :] = value.astype(BF16)


def column(row):
    size = row.shape[1]
    i = lax.broadcasted_iota(jnp.int32, (size, size), 0)
    j = lax.broadcasted_iota(jnp.int32, (size, size), 1)
    return jnp.sum(jnp.where(i == j, row, 0.0), axis=1, keepdims=True)


def repeated_eye(size, times):
    i = lax.broadcasted_iota(jnp.int32, (size, size), 0)
    j = lax.broadcasted_iota(jnp.int32, (size, size), 1)
    eye = jnp.where(i == j, 1.0, 0.0)
    return jnp.concatenate([eye] * times, axis=1).astype(BF16)


def body(
    shells,
    sectors,
    bricks,
    conv_w,
    conv_b,
    w1,
    b1,
    w2,
    queries,
    sample_src,
    depth_target,
    inten_target,
    drop_label,
    grad_bricks,
    ray_depth_out,
    reduced,
    sources,
    decoded,
    slope_conv,
    cols,
    cot_cols,
    cots,
    hot,
    hid_x,
    hid_t,
    own_table,
    tables,
    shell_buf,
    cell_send,
    cell_recv,
    pack,
    red_recv,
    table_sems,
    shell_sems,
    cell_sems,
    red_sems,
    out_sems,
):
    n = sectors
    count = shells * sectors
    nb, ch, cells = bricks.shape
    cap = queries.shape[1]
    hid = w1.shape[1]
    rays = sources.shape[1]
    groups = nb * cells // 256
    halves = cells // 256
    shell = lax.axis_index("shell")
    sector = lax.axis_index("sector")
    me = shell * n + sector
    lane = lax.broadcasted_iota(jnp.int32, (1, cells), 1)
    plane = lane >> 6

    def flat_peer(k):
        peer = lax.rem(me + k, count)
        return peer, {"shell": lax.div(peer, n), "sector": lax.rem(peer, n)}

    barrier = pltpu.get_barrier_semaphore()

    @pl.loop(1, count)
    def _(k):
        _, where = flat_peer(k)
        pl.semaphore_signal(barrier, inc=1, device_id=where, device_id_type=MESH)

    conv_b_col = column(conv_b[...])
    b1_col = column(b1[...])
    w2_density = column(w2[0:1, :])
    w2_intensity = column(w2[1:2, :])
    w1_t = matmul_nt(repeated_eye(hid, 1), w1[...]).astype(BF16)
    w1_rep = matmul(w1[...], repeated_eye(hid, 3)).astype(BF16)
    wide_w = conv_w[...].astype(F32)
    width = 9 * ch
    conv_rows = jnp.concatenate(
        [wide_w[:, a * width : (a + 1) * width] for a in range(3)], axis=0
    ).astype(BF16)
    turned = jnp.transpose(wide_w)
    back_rows = jnp.concatenate(
        [
            jnp.concatenate(
                [turned[(9 * a + 8 - k) * ch : (9 * a + 9 - k) * ch] for k in range(9)], axis=1
            )
            for a in range(3)
        ],
        axis=0,
    ).astype(BF16)
    block = SAMP * 128
    ray_of = lax.broadcasted_iota(jnp.int32, (block, 128), 0) // SAMP
    to_ray = jnp.where(ray_of == lax.broadcasted_iota(jnp.int32, (block, 128), 1), 1.0, 0.0)
    to_ray = to_ray.astype(BF16)
    sample_of = lax.broadcasted_iota(jnp.int32, (SAMP, block), 1) & (SAMP - 1)
    own_row = sample_of == lax.broadcasted_iota(jnp.int32, (SAMP, block), 0)
    for j in range(rays // 128):
        part = sample_src[:, j * block : (j + 1) * block]
        pair = [(part >> 7).astype(F32), (part & 127).astype(F32)]
        pair = jnp.concatenate([jnp.where(own_row, p, 0.0) for p in pair], axis=0)
        got = matmul(pair.astype(BF16), to_ray)
        whole = got[:SAMP] * 128.0 + got[SAMP:]
        sources[:, j * 128 : (j + 1) * 128] = whole.astype(jnp.int32)

    sig_density = []
    intensity_here = []
    for b in range(nb):
        unfold(bricks[b].astype(F32), cols.at[b], lane)
        by_a = matmul(conv_rows, cols[b])
        pre = conv_b_col
        for a in range(3):
            pre = pre + moved(by_a[a * ch : (a + 1) * ch], 64, plane, a - 1)
        value, slope = gelu_and_slope(pre)
        feats = value.astype(BF16)
        decoded[b] = feats
        slope_conv[b] = slope
        x = matmul(w1_t, feats) + b1_col
        t = jnp.tanh(GELU_SCALE * (x + GELU_CUBIC * (x * (x * x))))
        hid_x[b] = x
        hid_t[b] = t
        value = x * (0.5 * (1.0 + t))
        e0 = jnp.sum(value * w2_density, axis=0, keepdims=True)
        e1 = jnp.sum(value * w2_intensity, axis=0, keepdims=True)
        density = jnp.maximum(e0, 0.0) + jnp.log1p(jnp.exp(-jnp.abs(e0)))
        sig_density.append(1.0 / (1.0 + jnp.exp(-e0)))
        intensity_here.append(1.0 / (1.0 + jnp.exp(-e1)))
        for h in range(halves):
            row = b * halves + h
            at = slice(h * 256, (h + 1) * 256)
            own_table[row : row + 1, :] = density[:, at]
            own_table[groups + row : groups + row + 1, :] = intensity_here[b][:, at]

    pl.semaphore_wait(barrier, count - 1)

    def give_table(k):
        return pltpu.make_async_remote_copy(
            src_ref=own_table,
            dst_ref=tables.at[sector],
            send_sem=table_sems.at[0, k],
            recv_sem=table_sems.at[1, k],
            device_id={"shell": shell, "sector": lax.rem(sector + k, n)},
            device_id_type=MESH,
        )

    for k in range(1, n):
        give_table(k).start()
    tables[sector] = own_table[...]

    asked = queries[...]
    parts = cap // 256
    asked = jnp.concatenate([asked[:, h * 256 : (h + 1) * 256] for h in range(parts)], axis=0)
    asked = jnp.concatenate([(asked >> 6).astype(F32), (asked & 63).astype(F32)], axis=0)
    asked = asked.astype(BF16)
    held = parts * n
    place_of = lax.broadcasted_iota(jnp.int32, (256, rays), 0)
    held_of = lax.broadcasted_iota(jnp.int32, (held, rays), 0)
    codes = []
    for k in range(SAMP):
        src = sources[k : k + 1, :]
        owner = src >> (cap.bit_length() - 1)
        got = matmul(asked, jnp.where(place_of == (src & 255), 1.0, 0.0).astype(BF16))
        got = got[:held] * 64.0 + got[held:]
        mine = held_of == ((src >> 8) & (parts - 1)) * n + owner
        address = jnp.sum(jnp.where(mine, got, 0.0), axis=0, keepdims=True).astype(jnp.int32)
        hot[k] = jnp.where(place_of == (address & 255), 1.0, 0.0).astype(BF16)
        codes.append(owner * groups + (address >> 8))

    for k in range(1, n):
        give_table(k).wait()

    everything = tables[...].reshape(n * 2 * groups, 256)
    everything = jnp.concatenate([p.astype(BF16) for p in split(everything, 2)], axis=0)
    group_of = lax.broadcasted_iota(jnp.int32, (groups, rays), 0)
    total = n * 2 * groups
    dens = []
    inten = []
    for k in range(SAMP):
        got = matmul(everything, hot[k])
        got = got[:total] + got[total:]
        sums = [jnp.zeros((groups, rays), F32)] * 2
        for w in range(n):
            mine = group_of == codes[k] - w * groups
            for j in range(2):
                at = (2 * w + j) * groups
                sums[j] = sums[j] + jnp.where(mine, got[at : at + groups], 0.0)
        dens.append(jnp.sum(sums[0], axis=0, keepdims=True))
        inten.append(jnp.sum(sums[1], axis=0, keepdims=True))

    step_size = 2.0 / (shells * SAMP)
    span = 1.0 / (shells * SAMP)
    first = shell.astype(F32) * SAMP + 0.5
    before = jnp.zeros((1, rays), F32)
    depth = jnp.zeros((1, rays), F32)
    light = jnp.zeros((1, rays), F32)
    enter = []
    leave = []
    weight = []
    for k in range(SAMP):
        optical = dens[k] * step_size
        enter.append(jnp.exp(-before))
        leave.append(jnp.exp(-optical))
        weight.append(enter[k] * (1.0 - leave[k]))
        depth = depth + weight[k] * ((first + k) * span)
        light = light + weight[k] * inten[k]
        before = before + optical
    shell_buf[shell] = jnp.concatenate(
        [depth, light, before, jnp.zeros((5, rays), F32)], axis=0
    )

    def to_shell(k):
        return pltpu.make_async_remote_copy(
            src_ref=shell_buf.at[shell],
            dst_ref=shell_buf.at[shell],
            send_sem=shell_sems.at[0, k],
            recv_sem=shell_sems.at[1, k],
            device_id={"shell": lax.rem(shell + k, shells), "sector": sector},
            device_id_type=MESH,
        )

    for k in range(1, shells):
        to_shell(k).start()
    for b in range(nb):
        x = hid_x[b]
        t = hid_t[b]
        half = 0.5 * (1.0 + t)
        hid_x[b] = x * half
        hid_t[b] = half + 0.5 * x * (1.0 - t * t) * (
            GELU_SCALE * (1.0 + 3.0 * GELU_CUBIC * (x * x))
        )

    for k in range(1, shells):
        to_shell(k).wait()

    prefix = jnp.zeros((1, rays), F32)
    ray_depth = jnp.zeros((1, rays), F32)
    ray_light = jnp.zeros((1, rays), F32)
    entry = []
    for s in range(shells):
        entry.append(jnp.exp(-prefix))
        ray_depth = ray_depth + entry[s] * shell_buf[s, 0:1, :]
        ray_light = ray_light + entry[s] * shell_buf[s, 1:2, :]
        prefix = prefix + shell_buf[s, 2:3, :]
    ray_depth_out[...] = ray_depth
    escape = jnp.exp(-prefix)
    dropped = drop_label[...].astype(F32)
    kept = 1.0 - dropped
    off_depth = ray_depth - depth_target[...]
    off_light = ray_light - inten_target[...]
    off_escape = escape - dropped
    loss = jnp.sum(
        kept * (off_depth * off_depth + off_light * off_light) + off_escape * off_escape,
        axis=1,
        keepdims=True,
    )
    grad_depth = 2.0 * kept * off_depth
    grad_light = 2.0 * kept * off_light
    behind = jnp.zeros((1, rays), F32)
    own_entry = jnp.zeros((1, rays), F32)
    for s in range(shells):
        term = (grad_depth * shell_buf[s, 0:1, :] + grad_light * shell_buf[s, 1:2, :]) * entry[s]
        behind = behind + jnp.where(shell < s, term, 0.0)
        own_entry = own_entry + jnp.where(shell == s, entry[s], 0.0)
    cot_depth = grad_depth * own_entry
    cot_light = grad_light * own_entry
    cot_tau = -2.0 * off_escape * escape - behind
    later = jnp.zeros((1, rays), F32)
    dens_grad = [None] * SAMP
    inten_grad = [None] * SAMP
    for k in reversed(range(SAMP)):
        pull = cot_depth * ((first + k) * span) + cot_light * inten[k]
        inten_grad[k] = cot_light * weight[k]
        dens_grad[k] = step_size * (pull * enter[k] * leave[k] - later + cot_tau)
        later = later + pull * weight[k]

    table_grad = jnp.zeros((2 * total, 256), F32)
    for k in range(SAMP):
        masks = [group_of == codes[k] - w * groups for w in range(n)]
        pair = [split(dens_grad[k], 2), split(inten_grad[k], 2)]
        spread = jnp.concatenate(
            [
                jnp.where(masks[w], pair[j][p], 0.0).astype(BF16)
                for p in range(2)
                for w in range(n)
                for j in range(2)
            ],
            axis=0,
        )
        table_grad = table_grad + matmul_nt(spread, hot[k])
    table_grad = table_grad[:total] + table_grad[total:]
    cell_send[...] = table_grad.reshape(n, 2 * groups, 256)

    def give_back(k):
        peer = lax.rem(sector + k, n)
        return pltpu.make_async_remote_copy(
            src_ref=cell_send.at[peer],
            dst_ref=cell_recv.at[sector],
            send_sem=cell_sems.at[0, k],
            recv_sem=cell_sems.at[1, k],
            device_id={"shell": shell, "sector": peer},
            device_id_type=MESH,
        )

    for k in range(1, n):
        give_back(k).start()
    cell_recv[sector] = cell_send[sector]
    for k in range(1, n):
        give_back(k).wait()
    table_grad = jnp.sum(cell_recv[...], axis=0)

    w1_acc = jnp.zeros((ch, 3 * hid), F32)
    small = [jnp.zeros((hid, 1), F32)] * 3
    wgrad = jnp.zeros((3 * ch, width), F32)
    bias_grad = jnp.zeros((ch, 1), F32)
    for b in range(nb):
        rows = [
            jnp.concatenate(
                [
                    table_grad[j * groups + b * halves + h : j * groups + b * halves + h + 1]
                    for h in range(halves)
                ],
                axis=1,
            )
            for j in range(2)
        ]
        g0 = rows[0] * sig_density[b]
        g1 = rows[1] * (intensity_here[b] * (1.0 - intensity_here[b]))
        value = hid_x[b]
        grad = (w2_density * g0 + w2_intensity * g1) * hid_t[b]
        pieces = jnp.concatenate([p.astype(BF16) for p in split(grad, 3)], axis=0)
        w1_acc = w1_acc + matmul_nt(decoded[b], pieces)
        terms = (grad, value * g0, value * g1)
        small = [a + jnp.sum(t, axis=1, keepdims=True) for a, t in zip(small, terms)]
        cot = (matmul(w1_rep, pieces) * slope_conv[b]).astype(BF16)
        exact = cot.astype(F32)
        cots[b] = cot
        by_a = [moved(exact, 64, plane, 1 - a).astype(BF16) for a in range(3)]
        wgrad = wgrad + matmul_nt(jnp.concatenate(by_a, axis=0), cols[b])
        bias_grad = bias_grad + jnp.sum(exact, axis=1, keepdims=True)

    tiles = -(-27 * ch // 128)
    wgrad = jnp.concatenate(
        [wgrad[a * ch : (a + 1) * ch] for a in range(3)]
        + [jnp.zeros((ch, tiles * 128 - 27 * ch), F32)],
        axis=1,
    )
    for t in range(tiles):
        for part in range(ch // 8):
            pack[t * (ch // 8) + part] = wgrad[part * 8 : part * 8 + 8, t * 128 : t * 128 + 128]
    at_lane = lax.broadcasted_iota(jnp.int32, (ch, 128), 1)
    w1_grad = w1_acc[:, :hid] + w1_acc[:, hid : 2 * hid] + w1_acc[:, 2 * hid :]
    last = jnp.concatenate([w1_grad, jnp.zeros((ch, 128 - hid), F32)], axis=1)
    place = hid
    for j in range(3):
        for part in range(hid // ch):
            values = small[j][part * ch : (part + 1) * ch, :]
            last = last + jnp.where(at_lane == place, values, 0.0)
            place += 1
    last = last + jnp.where(at_lane == place, bias_grad, 0.0)
    loss_here = jnp.where(shell == 0, loss, 0.0)
    last = last + jnp.where(at_lane == place + 1, loss_here, 0.0)
    base = tiles * (ch // 8)
    for part in range(ch // 8):
        pack[base + part] = last[part * 8 : part * 8 + 8]
    for extra in range(base + ch // 8, pack.shape[0]):
        pack[extra] = jnp.zeros((8, 128), F32)

    def to_reducer(k):
        peer, where = flat_peer(k)
        return pltpu.make_async_remote_copy(
            src_ref=pack.at[peer],
            dst_ref=red_recv.at[me],
            send_sem=red_sems.at[0, k],
            recv_sem=red_sems.at[1, k],
            device_id=where,
            device_id_type=MESH,
        )

    def to_everyone(k):
        _, where = flat_peer(k)
        return pltpu.make_async_remote_copy(
            src_ref=reduced.at[me],
            dst_ref=reduced.at[me],
            send_sem=out_sems.at[0, k],
            recv_sem=out_sems.at[1, k],
            device_id=where,
            device_id_type=MESH,
        )

    @pl.loop(1, count)
    def _(k):
        to_reducer(k).start()

    red_recv[me] = pack[me]

    def brick_back(b):
        unfold(cots[b].astype(F32), cot_cols.at[b], lane)
        by_a = matmul(back_rows, cot_cols[b])
        grad = jnp.zeros((ch, cells), F32)
        for a in range(3):
            grad = grad + moved(by_a[a * ch : (a + 1) * ch], 64, plane, 1 - a)
        grad_bricks[b] = grad.astype(BF16)

    for b in range(nb // 2):
        brick_back(b)

    @pl.loop(1, count)
    def _(k):
        to_reducer(k).wait()

    reduced[me] = jnp.sum(red_recv[...], axis=0)

    @pl.loop(1, count)
    def _(k):
        to_everyone(k).start()

    for b in range(nb // 2, nb):
        brick_back(b)

    @pl.loop(1, count)
    def _(k):
        to_everyone(k).wait()


def finish(
    scale,
    reduced,
    grad_bricks,
    ray_depth,
    loss_out,
    conv_out,
    conv_b_out,
    w1_out,
    b1_out,
    w2_out,
    bricks_out,
    depth_out,
):
    ch, used = conv_out.shape
    hid = w1_out.shape[1]
    per = ch // 8
    tiles = -(-used // 128)
    for t in range(tiles):
        stop = min(128, used - t * 128)
        for part in range(per):
            conv_out[part * 8 : part * 8 + 8, t * 128 : t * 128 + stop] = reduced[
                t * per + part, :, :stop
            ]
    last = jnp.concatenate([reduced[tiles * per + part] for part in range(per)], axis=0)
    w1_out[...] = last[:, :hid]

    def row(place, count):
        i = lax.broadcasted_iota(jnp.int32, (ch, ch * count), 0)
        j = lax.broadcasted_iota(jnp.int32, (ch, ch * count), 1)
        total = jnp.zeros((1, ch * count), F32)
        for part in range(count):
            spread = jnp.where(j == i + part * ch, last[:, place + part : place + part + 1], 0.0)
            total = total + jnp.sum(spread, axis=0, keepdims=True)
        return total

    count = hid // ch
    b1_out[...] = row(hid, count)
    w2_out[0:1, :] = row(hid + count, count)
    w2_out[1:2, :] = row(hid + 2 * count, count)
    place = hid + 3 * count
    conv_b_out[...] = row(place, 1)
    loss_out[...] = last[0:1, place + 1 : place + 2] * scale
    bricks_out[...] = grad_bricks[...]
    depth_out[...] = ray_depth[...]


def local(
    bricks,
    conv_w,
    conv_b,
    head_w1,
    head_b1,
    head_w2,
    queries,
    sample_src,
    depth_target,
    inten_target,
    drop_label,
):
    shells = lax.axis_size("shell")
    n = lax.axis_size("sector")
    count = shells * n
    _, nb, ch, cells = bricks.shape
    cap = queries.shape[2]
    hid = head_w1.shape[1]
    rays = depth_target.shape[0]
    groups = nb * cells // 256
    chunks = (-(-27 * ch // 128) + 1) * (ch // 8)
    assert chunks <= count and cap & (cap - 1) == 0 and cap >= 256 and cells == 512 and rays % 128 == 0
    operands = (
        bricks[0],
        conv_w,
        conv_b[None],
        head_w1,
        head_b1[None],
        head_w2.T,
        queries[0],
        sample_src,
        depth_target[None],
        inten_target[None],
        drop_label[None],
    )
    vmem = pl.BlockSpec(memory_space=pltpu.VMEM)
    dma = pltpu.SemaphoreType.DMA
    grad_bricks, ray_depth, reduced = pl.pallas_call(
        functools.partial(body, shells, n),
        out_shape=(
            jax.ShapeDtypeStruct((nb, ch, cells), BF16),
            jax.ShapeDtypeStruct((1, rays), F32),
            jax.ShapeDtypeStruct((count, 8, 128), F32),
        ),
        in_specs=[vmem] * len(operands),
        out_specs=(vmem, vmem, vmem),
        scratch_shapes=[
            pltpu.VMEM((SAMP, rays), jnp.int32),
            pltpu.VMEM((nb, ch, cells), BF16),
            pltpu.VMEM((nb, ch, cells), F32),
            pltpu.VMEM((nb, 9 * ch, cells), BF16),
            pltpu.VMEM((nb, 9 * ch, cells), BF16),
            pltpu.VMEM((nb, ch, cells), BF16),
            pltpu.VMEM((SAMP, 256, rays), BF16),
            pltpu.VMEM((nb, hid, cells), F32),
            pltpu.VMEM((nb, hid, cells), F32),
            pltpu.VMEM((2 * groups, 256), F32),
            pltpu.VMEM((n, 2 * groups, 256), F32),
            pltpu.VMEM((shells, 8, rays), F32),
            pltpu.VMEM((n, 2 * groups, 256), F32),
            pltpu.VMEM((n, 2 * groups, 256), F32),
            pltpu.VMEM((count, 8, 128), F32),
            pltpu.VMEM((count, 8, 128), F32),
            dma((2, n)),
            dma((2, shells)),
            dma((2, n)),
            dma((2, count)),
            dma((2, count)),
        ],
        compiler_params=pltpu.CompilerParams(
            collective_id=0, has_side_effects=True, vmem_limit_bytes=56 * 1024 * 1024
        ),
    )(*operands)
    loss, conv_grad, conv_b_grad, w1_grad, b1_grad, w2_grad, grad_bricks, ray_depth = pl.pallas_call(
        functools.partial(finish, 1.0 / (rays * n)),
        out_shape=(
            jax.ShapeDtypeStruct((1, 1), F32),
            jax.ShapeDtypeStruct((ch, 27 * ch), F32),
            jax.ShapeDtypeStruct((1, ch), F32),
            jax.ShapeDtypeStruct((ch, hid), F32),
            jax.ShapeDtypeStruct((1, hid), F32),
            jax.ShapeDtypeStruct((2, hid), F32),
            jax.ShapeDtypeStruct((nb, ch, cells), BF16),
            jax.ShapeDtypeStruct((1, rays), F32),
        ),
        in_specs=[vmem] * 3,
        out_specs=(vmem,) * 8,
    )(reduced, grad_bricks, ray_depth)
    return (
        loss[0, 0],
        conv_grad,
        conv_b_grad[0],
        w1_grad,
        b1_grad[0],
        w2_grad.T,
        grad_bricks[None],
        ray_depth[0],
    )


def solution(mesh):
    return jax.shard_map(
        local,
        mesh=mesh,
        in_specs=(
            P("shell", "sector", None, None),
            P(),
            P(),
            P(),
            P(),
            P(),
            P("shell", "sector", None),
            P("shell", "sector"),
            P("sector"),
            P("sector"),
            P("sector"),
        ),
        out_specs=(P(), P(), P(), P(), P(), P(), P("shell", "sector", None, None), P("sector")),
        check_vma=False,
    )
```

```python
import functools
import math

import jax
import jax.numpy as jnp
from jax import lax
from jax.experimental import pallas as pl
from jax.experimental.pallas import tpu as pltpu
from jax.sharding import PartitionSpec as P

SAMP = 8
MESH = pl.DeviceIdType.MESH
F32 = jnp.float32
BF16 = jnp.bfloat16
GELU_SCALE = math.sqrt(2.0 / math.pi)
GELU_CUBIC = 0.044715
NT = (((1,), (1,)), ((), ()))


def gelu_and_slope(x):
    square = x * x
    t = jnp.tanh(GELU_SCALE * (x + GELU_CUBIC * (x * square)))
    half = 0.5 * (1.0 + t)
    slope = half + 0.5 * x * (1.0 - t * t) * (GELU_SCALE * (1.0 + 3.0 * GELU_CUBIC * square))
    return x * half, slope


def split(value, count):
    pieces = []
    for _ in range(count - 1):
        piece = value.astype(BF16).astype(F32)
        pieces.append(piece)
        value = value - piece
    return pieces + [value]


def matmul(a, b):
    return jnp.dot(a, b, preferred_element_type=F32)


def matmul_nt(a, b):
    return lax.dot_general(a, b, NT, preferred_element_type=F32)


def moved(x, step, coord, move):
    if move == 0:
        return x
    rolled = pltpu.roll(x, (-move * step) % x.shape[1], 1)
    inside = coord >= 1 if move < 0 else coord <= 6
    return rolled * jnp.where(inside, 1.0, 0.0)


def unfold(x, out, lane):
    ch = x.shape[0]
    for c in range(3):
        by_c = moved(x, 1, lane & 7, c - 1)
        for b in range(3):
            k = 3 * b + c
            value = moved(by_c, 8, (lane >> 3) & 7, b - 1)
            out[k * ch : (k + 1) * ch, :] = value.astype(BF16)


def column(row):
    size = row.shape[1]
    i = lax.broadcasted_iota(jnp.int32, (size, size), 0)
    j = lax.broadcasted_iota(jnp.int32, (size, size), 1)
    return jnp.sum(jnp.where(i == j, row, 0.0), axis=1, keepdims=True)


def repeated_eye(size, times):
    i = lax.broadcasted_iota(jnp.int32, (size, size), 0)
    j = lax.broadcasted_iota(jnp.int32, (size, size), 1)
    eye = jnp.where(i == j, 1.0, 0.0)
    return jnp.concatenate([eye] * times, axis=1).astype(BF16)


def body(
    shells,
    sectors,
    bricks,
    conv_w,
    conv_b,
    w1,
    b1,
    w2,
    queries,
    sample_src,
    depth_target,
    inten_target,
    drop_label,
    grad_bricks,
    ray_depth_out,
    reduced,
    sources,
    decoded,
    slope_conv,
    cols,
    cot_cols,
    cots,
    hot,
    hid_x,
    hid_t,
    own_table,
    tables,
    shell_buf,
    cell_send,
    cell_recv,
    pack,
    red_recv,
    table_sems,
    shell_sems,
    cell_sems,
    red_sems,
    out_sems,
):
    n = sectors
    count = shells * sectors
    nb, ch, cells = bricks.shape
    cap = queries.shape[1]
    hid = w1.shape[1]
    rays = sources.shape[1]
    groups = nb * cells // 256
    halves = cells // 256
    shell = lax.axis_index("shell")
    sector = lax.axis_index("sector")
    me = shell * n + sector
    lane = lax.broadcasted_iota(jnp.int32, (1, cells), 1)
    plane = lane >> 6

    shell_after = [shell] + [lax.rem(shell + k, shells) for k in range(1, shells)]
    sector_after = [sector] + [lax.rem(sector + k, n) for k in range(1, n)]

    def flat_peer(k):
        to_shell, to_sector = shell_after[k // n], sector_after[k % n]
        return to_shell * n + to_sector, {"shell": to_shell, "sector": to_sector}

    barrier = pltpu.get_barrier_semaphore()
    for k in range(1, count):
        _, where = flat_peer(k)
        pl.semaphore_signal(barrier, inc=1, device_id=where, device_id_type=MESH)

    conv_b_col = column(conv_b[...])
    b1_col = column(b1[...])
    w2_density = column(w2[0:1, :])
    w2_intensity = column(w2[1:2, :])
    w1_t = matmul_nt(repeated_eye(hid, 1), w1[...]).astype(BF16)
    wide_w = conv_w[...].astype(F32)
    width = 9 * ch
    conv_rows = jnp.concatenate(
        [wide_w[:, a * width : (a + 1) * width] for a in range(3)], axis=0
    ).astype(BF16)
    block = SAMP * 128
    ray_of = lax.broadcasted_iota(jnp.int32, (block, 128), 0) // SAMP
    to_ray = jnp.where(ray_of == lax.broadcasted_iota(jnp.int32, (block, 128), 1), 1.0, 0.0)
    to_ray = to_ray.astype(BF16)
    sample_of = lax.broadcasted_iota(jnp.int32, (SAMP, block), 1) & (SAMP - 1)
    own_row = sample_of == lax.broadcasted_iota(jnp.int32, (SAMP, block), 0)
    for j in range(rays // 128):
        part = sample_src[:, j * block : (j + 1) * block]
        pair = [(part >> 7).astype(F32), (part & 127).astype(F32)]
        pair = jnp.concatenate([jnp.where(own_row, p, 0.0) for p in pair], axis=0)
        got = matmul(pair.astype(BF16), to_ray)
        whole = got[:SAMP] * 128.0 + got[SAMP:]
        sources[:, j * 128 : (j + 1) * 128] = whole.astype(jnp.int32)

    sig_density = []
    intensity_here = []
    for b in range(nb):
        unfold(bricks[b].astype(F32), cols.at[b], lane)
        by_a = matmul(conv_rows, cols[b])
        pre = conv_b_col
        for a in range(3):
            pre = pre + moved(by_a[a * ch : (a + 1) * ch], 64, plane, a - 1)
        value, slope = gelu_and_slope(pre)
        feats = value.astype(BF16)
        decoded[b] = feats
        slope_conv[b] = slope
        x = matmul(w1_t, feats) + b1_col
        t = jnp.tanh(GELU_SCALE * (x + GELU_CUBIC * (x * (x * x))))
        hid_x[b] = x
        hid_t[b] = t
        value = x * (0.5 * (1.0 + t))
        e0 = jnp.sum(value * w2_density, axis=0, keepdims=True)
        e1 = jnp.sum(value * w2_intensity, axis=0, keepdims=True)
        density = jnp.maximum(e0, 0.0) + jnp.log1p(jnp.exp(-jnp.abs(e0)))
        sig_density.append(1.0 / (1.0 + jnp.exp(-e0)))
        intensity_here.append(1.0 / (1.0 + jnp.exp(-e1)))
        for h in range(halves):
            row = b * halves + h
            at = slice(h * 256, (h + 1) * 256)
            own_table[row : row + 1, :] = density[:, at]
            own_table[groups + row : groups + row + 1, :] = intensity_here[b][:, at]

    pl.semaphore_wait(barrier, count - 1)

    def give_table(k):
        return pltpu.make_async_remote_copy(
            src_ref=own_table,
            dst_ref=tables.at[sector],
            send_sem=table_sems.at[0, k],
            recv_sem=table_sems.at[1, k],
            device_id={"shell": shell, "sector": sector_after[k]},
            device_id_type=MESH,
        )

    for k in range(1, n):
        give_table(k).start()
    tables[sector] = own_table[...]

    asked = queries[...]
    parts = cap // 256
    asked = jnp.concatenate([asked[:, h * 256 : (h + 1) * 256] for h in range(parts)], axis=0)
    asked = jnp.concatenate([(asked >> 6).astype(F32), (asked & 63).astype(F32)], axis=0)
    asked = asked.astype(BF16)
    held = parts * n
    place_of = lax.broadcasted_iota(jnp.int32, (256, rays), 0)
    held_of = lax.broadcasted_iota(jnp.int32, (held, rays), 0)
    codes = []
    for k in range(SAMP):
        src = sources[k : k + 1, :]
        owner = src >> (cap.bit_length() - 1)
        got = matmul(asked, jnp.where(place_of == (src & 255), 1.0, 0.0).astype(BF16))
        got = got[:held] * 64.0 + got[held:]
        mine = held_of == ((src >> 8) & (parts - 1)) * n + owner
        address = jnp.sum(jnp.where(mine, got, 0.0), axis=0, keepdims=True).astype(jnp.int32)
        hot[k] = jnp.where(place_of == (address & 255), 1.0, 0.0).astype(BF16)
        codes.append(owner * groups + (address >> 8))

    for k in range(1, n):
        give_table(k).wait()

    everything = tables[...].reshape(n * 2 * groups, 256)
    everything = jnp.concatenate([p.astype(BF16) for p in split(everything, 2)], axis=0)
    group_of = lax.broadcasted_iota(jnp.int32, (groups, rays), 0)
    total = n * 2 * groups
    dens = []
    inten = []
    for k in range(SAMP):
        got = matmul(everything, hot[k])
        got = got[:total] + got[total:]
        sums = [jnp.zeros((groups, rays), F32)] * 2
        for w in range(n):
            mine = group_of == codes[k] - w * groups
            for j in range(2):
                at = (2 * w + j) * groups
                sums[j] = sums[j] + jnp.where(mine, got[at : at + groups], 0.0)
        dens.append(jnp.sum(sums[0], axis=0, keepdims=True))
        inten.append(jnp.sum(sums[1], axis=0, keepdims=True))

    step_size = 2.0 / (shells * SAMP)
    span = 1.0 / (shells * SAMP)
    first = shell.astype(F32) * SAMP + 0.5
    before = jnp.zeros((1, rays), F32)
    depth = jnp.zeros((1, rays), F32)
    light = jnp.zeros((1, rays), F32)
    enter = []
    leave = []
    weight = []
    for k in range(SAMP):
        optical = dens[k] * step_size
        enter.append(jnp.exp(-before))
        leave.append(jnp.exp(-optical))
        weight.append(enter[k] * (1.0 - leave[k]))
        depth = depth + weight[k] * ((first + k) * span)
        light = light + weight[k] * inten[k]
        before = before + optical
    shell_buf[shell] = jnp.concatenate(
        [depth, light, before, jnp.zeros((5, rays), F32)], axis=0
    )

    def to_shell(k):
        return pltpu.make_async_remote_copy(
            src_ref=shell_buf.at[shell],
            dst_ref=shell_buf.at[shell],
            send_sem=shell_sems.at[0, k],
            recv_sem=shell_sems.at[1, k],
            device_id={"shell": shell_after[k], "sector": sector},
            device_id_type=MESH,
        )

    for k in range(1, shells):
        to_shell(k).start()
    for b in range(nb):
        x = hid_x[b]
        t = hid_t[b]
        half = 0.5 * (1.0 + t)
        hid_x[b] = x * half
        hid_t[b] = half + 0.5 * x * (1.0 - t * t) * (
            GELU_SCALE * (1.0 + 3.0 * GELU_CUBIC * (x * x))
        )

    for k in range(1, shells):
        to_shell(k).wait()

    prefix = jnp.zeros((1, rays), F32)
    ray_depth = jnp.zeros((1, rays), F32)
    ray_light = jnp.zeros((1, rays), F32)
    entry = []
    for s in range(shells):
        entry.append(jnp.exp(-prefix))
        ray_depth = ray_depth + entry[s] * shell_buf[s, 0:1, :]
        ray_light = ray_light + entry[s] * shell_buf[s, 1:2, :]
        prefix = prefix + shell_buf[s, 2:3, :]
    ray_depth_out[...] = ray_depth
    escape = jnp.exp(-prefix)
    dropped = drop_label[...].astype(F32)
    kept = 1.0 - dropped
    off_depth = ray_depth - depth_target[...]
    off_light = ray_light - inten_target[...]
    off_escape = escape - dropped
    loss = jnp.sum(
        kept * (off_depth * off_depth + off_light * off_light) + off_escape * off_escape,
        axis=1,
        keepdims=True,
    )
    grad_depth = 2.0 * kept * off_depth
    grad_light = 2.0 * kept * off_light
    behind = jnp.zeros((1, rays), F32)
    own_entry = jnp.zeros((1, rays), F32)
    for s in range(shells):
        term = (grad_depth * shell_buf[s, 0:1, :] + grad_light * shell_buf[s, 1:2, :]) * entry[s]
        behind = behind + jnp.where(shell < s, term, 0.0)
        own_entry = own_entry + jnp.where(shell == s, entry[s], 0.0)
    cot_depth = grad_depth * own_entry
    cot_light = grad_light * own_entry
    cot_tau = -2.0 * off_escape * escape - behind
    later = jnp.zeros((1, rays), F32)
    dens_grad = [None] * SAMP
    inten_grad = [None] * SAMP
    for k in reversed(range(SAMP)):
        pull = cot_depth * ((first + k) * span) + cot_light * inten[k]
        inten_grad[k] = cot_light * weight[k]
        dens_grad[k] = step_size * (pull * enter[k] * leave[k] - later + cot_tau)
        later = later + pull * weight[k]

    table_grad = jnp.zeros((2 * total, 256), F32)
    for k in range(SAMP):
        masks = [group_of == codes[k] - w * groups for w in range(n)]
        pair = [split(dens_grad[k], 2), split(inten_grad[k], 2)]
        spread = jnp.concatenate(
            [
                jnp.where(masks[w], pair[j][p], 0.0).astype(BF16)
                for p in range(2)
                for w in range(n)
                for j in range(2)
            ],
            axis=0,
        )
        table_grad = table_grad + matmul_nt(spread, hot[k])
    table_grad = table_grad[:total] + table_grad[total:]
    cell_send[...] = table_grad.reshape(n, 2 * groups, 256)

    def give_back(k):
        peer = sector_after[k]
        return pltpu.make_async_remote_copy(
            src_ref=cell_send.at[peer],
            dst_ref=cell_recv.at[sector],
            send_sem=cell_sems.at[0, k],
            recv_sem=cell_sems.at[1, k],
            device_id={"shell": shell, "sector": peer},
            device_id_type=MESH,
        )

    for k in range(1, n):
        give_back(k).start()
    cell_recv[sector] = cell_send[sector]
    w1_rep = matmul(w1[...], repeated_eye(hid, 3)).astype(BF16)
    turned = jnp.transpose(wide_w)
    back_rows = jnp.concatenate(
        [
            jnp.concatenate(
                [turned[(9 * a + 8 - k) * ch : (9 * a + 9 - k) * ch] for k in range(9)], axis=1
            )
            for a in range(3)
        ],
        axis=0,
    ).astype(BF16)
    for k in range(1, n):
        give_back(k).wait()
    table_grad = jnp.sum(cell_recv[...], axis=0)

    w1_acc = jnp.zeros((ch, 3 * hid), F32)
    small = [jnp.zeros((hid, 1), F32)] * 3
    wgrad = jnp.zeros((3 * ch, width), F32)
    bias_grad = jnp.zeros((ch, 1), F32)
    for b in range(nb):
        rows = [
            jnp.concatenate(
                [
                    table_grad[j * groups + b * halves + h : j * groups + b * halves + h + 1]
                    for h in range(halves)
                ],
                axis=1,
            )
            for j in range(2)
        ]
        g0 = rows[0] * sig_density[b]
        g1 = rows[1] * (intensity_here[b] * (1.0 - intensity_here[b]))
        value = hid_x[b]
        grad = (w2_density * g0 + w2_intensity * g1) * hid_t[b]
        pieces = jnp.concatenate([p.astype(BF16) for p in split(grad, 3)], axis=0)
        w1_acc = w1_acc + matmul_nt(decoded[b], pieces)
        terms = (grad, value * g0, value * g1)
        small = [a + jnp.sum(t, axis=1, keepdims=True) for a, t in zip(small, terms)]
        cot = (matmul(w1_rep, pieces) * slope_conv[b]).astype(BF16)
        exact = cot.astype(F32)
        cots[b] = cot
        by_a = [moved(exact, 64, plane, 1 - a).astype(BF16) for a in range(3)]
        wgrad = wgrad + matmul_nt(jnp.concatenate(by_a, axis=0), cols[b])
        bias_grad = bias_grad + jnp.sum(exact, axis=1, keepdims=True)

    tiles = -(-27 * ch // 128)
    wgrad = jnp.concatenate(
        [wgrad[a * ch : (a + 1) * ch] for a in range(3)]
        + [jnp.zeros((ch, tiles * 128 - 27 * ch), F32)],
        axis=1,
    )
    for t in range(tiles):
        for part in range(ch // 8):
            pack[t * (ch // 8) + part] = wgrad[part * 8 : part * 8 + 8, t * 128 : t * 128 + 128]
    at_lane = lax.broadcasted_iota(jnp.int32, (ch, 128), 1)
    w1_grad = w1_acc[:, :hid] + w1_acc[:, hid : 2 * hid] + w1_acc[:, 2 * hid :]
    last = jnp.concatenate([w1_grad, jnp.zeros((ch, 128 - hid), F32)], axis=1)
    place = hid
    for j in range(3):
        for part in range(hid // ch):
            values = small[j][part * ch : (part + 1) * ch, :]
            last = last + jnp.where(at_lane == place, values, 0.0)
            place += 1
    last = last + jnp.where(at_lane == place, bias_grad, 0.0)
    loss_here = jnp.where(shell == 0, loss, 0.0)
    last = last + jnp.where(at_lane == place + 1, loss_here, 0.0)
    base = tiles * (ch // 8)
    for part in range(ch // 8):
        pack[base + part] = last[part * 8 : part * 8 + 8]
    for extra in range(base + ch // 8, pack.shape[0]):
        pack[extra] = jnp.zeros((8, 128), F32)

    def to_reducer(k):
        peer, where = flat_peer(k)
        return pltpu.make_async_remote_copy(
            src_ref=pack.at[peer],
            dst_ref=red_recv.at[me],
            send_sem=red_sems.at[0, k],
            recv_sem=red_sems.at[1, k],
            device_id=where,
            device_id_type=MESH,
        )

    def to_everyone(k):
        _, where = flat_peer(k)
        return pltpu.make_async_remote_copy(
            src_ref=reduced.at[me],
            dst_ref=reduced.at[me],
            send_sem=out_sems.at[0, k],
            recv_sem=out_sems.at[1, k],
            device_id=where,
            device_id_type=MESH,
        )

    for k in range(1, count):
        to_reducer(k).start()

    red_recv[me] = pack[me]

    def brick_back(b):
        unfold(cots[b].astype(F32), cot_cols.at[b], lane)
        by_a = matmul(back_rows, cot_cols[b])
        grad = jnp.zeros((ch, cells), F32)
        for a in range(3):
            grad = grad + moved(by_a[a * ch : (a + 1) * ch], 64, plane, 1 - a)
        grad_bricks[b] = grad.astype(BF16)

    for b in range(nb // 2):
        brick_back(b)

    for k in range(1, count):
        to_reducer(k).wait()

    reduced[me] = jnp.sum(red_recv[...], axis=0)

    for k in range(1, count):
        to_everyone(k).start()

    for b in range(nb // 2, nb):
        brick_back(b)

    for k in range(1, count):
        to_everyone(k).wait()


def finish(
    scale,
    reduced,
    grad_bricks,
    ray_depth,
    loss_out,
    conv_out,
    conv_b_out,
    w1_out,
    b1_out,
    w2_out,
    bricks_out,
    depth_out,
):
    ch, used = conv_out.shape
    hid = w1_out.shape[1]
    per = ch // 8
    tiles = -(-used // 128)
    for t in range(tiles):
        stop = min(128, used - t * 128)
        for part in range(per):
            conv_out[part * 8 : part * 8 + 8, t * 128 : t * 128 + stop] = reduced[
                t * per + part, :, :stop
            ]
    last = jnp.concatenate([reduced[tiles * per + part] for part in range(per)], axis=0)
    w1_out[...] = last[:, :hid]

    def row(place, count):
        i = lax.broadcasted_iota(jnp.int32, (ch, ch * count), 0)
        j = lax.broadcasted_iota(jnp.int32, (ch, ch * count), 1)
        total = jnp.zeros((1, ch * count), F32)
        for part in range(count):
            spread = jnp.where(j == i + part * ch, last[:, place + part : place + part + 1], 0.0)
            total = total + jnp.sum(spread, axis=0, keepdims=True)
        return total

    count = hid // ch
    b1_out[...] = row(hid, count)
    w2_out[0:1, :] = row(hid + count, count)
    w2_out[1:2, :] = row(hid + 2 * count, count)
    place = hid + 3 * count
    conv_b_out[...] = row(place, 1)
    loss_out[...] = last[0:1, place + 1 : place + 2] * scale
    bricks_out[...] = grad_bricks[...]
    depth_out[...] = ray_depth[...]


def local(
    bricks,
    conv_w,
    conv_b,
    head_w1,
    head_b1,
    head_w2,
    queries,
    sample_src,
    depth_target,
    inten_target,
    drop_label,
):
    shells = lax.axis_size("shell")
    n = lax.axis_size("sector")
    count = shells * n
    _, nb, ch, cells = bricks.shape
    cap = queries.shape[2]
    hid = head_w1.shape[1]
    rays = depth_target.shape[0]
    groups = nb * cells // 256
    chunks = (-(-27 * ch // 128) + 1) * (ch // 8)
    assert chunks <= count and cap & (cap - 1) == 0 and cap >= 256 and cells == 512 and rays % 128 == 0
    operands = (
        bricks[0],
        conv_w,
        conv_b[None],
        head_w1,
        head_b1[None],
        head_w2.T,
        queries[0],
        sample_src,
        depth_target[None],
        inten_target[None],
        drop_label[None],
    )
    vmem = pl.BlockSpec(memory_space=pltpu.VMEM)
    dma = pltpu.SemaphoreType.DMA
    grad_bricks, ray_depth, reduced = pl.pallas_call(
        functools.partial(body, shells, n),
        out_shape=(
            jax.ShapeDtypeStruct((nb, ch, cells), BF16),
            jax.ShapeDtypeStruct((1, rays), F32),
            jax.ShapeDtypeStruct((count, 8, 128), F32),
        ),
        in_specs=[vmem] * len(operands),
        out_specs=(vmem, vmem, vmem),
        scratch_shapes=[
            pltpu.VMEM((SAMP, rays), jnp.int32),
            pltpu.VMEM((nb, ch, cells), BF16),
            pltpu.VMEM((nb, ch, cells), F32),
            pltpu.VMEM((nb, 9 * ch, cells), BF16),
            pltpu.VMEM((nb, 9 * ch, cells), BF16),
            pltpu.VMEM((nb, ch, cells), BF16),
            pltpu.VMEM((SAMP, 256, rays), BF16),
            pltpu.VMEM((nb, hid, cells), F32),
            pltpu.VMEM((nb, hid, cells), F32),
            pltpu.VMEM((2 * groups, 256), F32),
            pltpu.VMEM((n, 2 * groups, 256), F32),
            pltpu.VMEM((shells, 8, rays), F32),
            pltpu.VMEM((n, 2 * groups, 256), F32),
            pltpu.VMEM((n, 2 * groups, 256), F32),
            pltpu.VMEM((count, 8, 128), F32),
            pltpu.VMEM((count, 8, 128), F32),
            dma((2, n)),
            dma((2, shells)),
            dma((2, n)),
            dma((2, count)),
            dma((2, count)),
        ],
        compiler_params=pltpu.CompilerParams(
            collective_id=0, has_side_effects=True, vmem_limit_bytes=56 * 1024 * 1024
        ),
    )(*operands)
    loss, conv_grad, conv_b_grad, w1_grad, b1_grad, w2_grad, grad_bricks, ray_depth = pl.pallas_call(
        functools.partial(finish, 1.0 / (rays * n)),
        out_shape=(
            jax.ShapeDtypeStruct((1, 1), F32),
            jax.ShapeDtypeStruct((ch, 27 * ch), F32),
            jax.ShapeDtypeStruct((1, ch), F32),
            jax.ShapeDtypeStruct((ch, hid), F32),
            jax.ShapeDtypeStruct((1, hid), F32),
            jax.ShapeDtypeStruct((2, hid), F32),
            jax.ShapeDtypeStruct((nb, ch, cells), BF16),
            jax.ShapeDtypeStruct((1, rays), F32),
        ),
        in_specs=[vmem] * 3,
        out_specs=(vmem,) * 8,
    )(reduced, grad_bricks, ray_depth)
    return (
        loss[0, 0],
        conv_grad,
        conv_b_grad[0],
        w1_grad,
        b1_grad[0],
        w2_grad.T,
        grad_bricks[None],
        ray_depth[0],
    )


def solution(mesh):
    return jax.shard_map(
        local,
        mesh=mesh,
        in_specs=(
            P("shell", "sector", None, None),
            P(),
            P(),
            P(),
            P(),
            P(),
            P("shell", "sector", None),
            P("shell", "sector"),
            P("sector"),
            P("sector"),
            P("sector"),
        ),
        out_specs=(P(), P(), P(), P(), P(), P(), P("shell", "sector", None, None), P("sector")),
        check_vma=False,
    )
```

```python
import functools
import math

import jax
import jax.numpy as jnp
from jax import lax
from jax.experimental import pallas as pl
from jax.experimental.pallas import tpu as pltpu
from jax.sharding import PartitionSpec as P

SAMP = 8
MESH = pl.DeviceIdType.MESH
F32 = jnp.float32
BF16 = jnp.bfloat16
GELU_SCALE = math.sqrt(2.0 / math.pi)
GELU_CUBIC = 0.044715
NT = (((1,), (1,)), ((), ()))


def gelu_and_slope(x):
    square = x * x
    t = jnp.tanh(GELU_SCALE * (x + GELU_CUBIC * (x * square)))
    half = 0.5 * (1.0 + t)
    slope = half + 0.5 * x * (1.0 - t * t) * (GELU_SCALE * (1.0 + 3.0 * GELU_CUBIC * square))
    return x * half, slope


def split(value, count):
    pieces = []
    for _ in range(count - 1):
        piece = value.astype(BF16).astype(F32)
        pieces.append(piece)
        value = value - piece
    return pieces + [value]


def matmul(a, b):
    return jnp.dot(a, b, preferred_element_type=F32)


def matmul_nt(a, b):
    return lax.dot_general(a, b, NT, preferred_element_type=F32)


def moved(x, step, coord, move):
    if move == 0:
        return x
    rolled = pltpu.roll(x, (-move * step) % x.shape[1], 1)
    inside = coord >= 1 if move < 0 else coord <= 6
    return rolled * jnp.where(inside, 1.0, 0.0)


def unfold(x, out, lane):
    ch = x.shape[0]
    for c in range(3):
        by_c = moved(x, 1, lane & 7, c - 1)
        for b in range(3):
            k = 3 * b + c
            value = moved(by_c, 8, (lane >> 3) & 7, b - 1)
            out[k * ch : (k + 1) * ch, :] = value.astype(BF16)


def column(row):
    size = row.shape[1]
    i = lax.broadcasted_iota(jnp.int32, (size, size), 0)
    j = lax.broadcasted_iota(jnp.int32, (size, size), 1)
    return jnp.sum(jnp.where(i == j, row, 0.0), axis=1, keepdims=True)


def repeated_eye(size, times):
    i = lax.broadcasted_iota(jnp.int32, (size, size), 0)
    j = lax.broadcasted_iota(jnp.int32, (size, size), 1)
    eye = jnp.where(i == j, 1.0, 0.0)
    return jnp.concatenate([eye] * times, axis=1).astype(BF16)


def body(
    shells,
    sectors,
    bricks,
    conv_w,
    conv_b,
    w1,
    b1,
    w2,
    queries,
    sample_src,
    depth_target,
    inten_target,
    drop_label,
    grad_bricks,
    ray_depth_out,
    reduced,
    sources,
    decoded,
    slope_conv,
    cols,
    cot_cols,
    cots,
    hot,
    hid_x,
    hid_t,
    own_table,
    tables,
    shell_buf,
    cell_send,
    cell_recv,
    pack,
    red_recv,
    table_sems,
    shell_sems,
    cell_sems,
    red_sems,
    out_sems,
):
    n = sectors
    count = shells * sectors
    nb, ch, cells = bricks.shape
    cap = queries.shape[1]
    hid = w1.shape[1]
    rays = sources.shape[1]
    groups = nb * cells // 256
    halves = cells // 256
    shell = lax.axis_index("shell")
    sector = lax.axis_index("sector")
    me = shell * n + sector
    lane = lax.broadcasted_iota(jnp.int32, (1, cells), 1)
    plane = lane >> 6

    shell_after = [shell] + [lax.rem(shell + k, shells) for k in range(1, shells)]
    sector_after = [sector] + [lax.rem(sector + k, n) for k in range(1, n)]

    def flat_peer(k):
        to_shell, to_sector = shell_after[k // n], sector_after[k % n]
        return to_shell * n + to_sector, {"shell": to_shell, "sector": to_sector}

    barrier = pltpu.get_barrier_semaphore()
    for k in range(1, count):
        _, where = flat_peer(k)
        pl.semaphore_signal(barrier, inc=1, device_id=where, device_id_type=MESH)

    conv_b_col = column(conv_b[...])
    b1_col = column(b1[...])
    w2_density = column(w2[0:1, :])
    w2_intensity = column(w2[1:2, :])
    w1_t = matmul_nt(repeated_eye(hid, 1), w1[...]).astype(BF16)
    wide_w = conv_w[...].astype(F32)
    width = 9 * ch
    conv_rows = jnp.concatenate(
        [wide_w[:, a * width : (a + 1) * width] for a in range(3)], axis=0
    ).astype(BF16)
    block = SAMP * 128
    ray_of = lax.broadcasted_iota(jnp.int32, (block, 128), 0) // SAMP
    to_ray = jnp.where(ray_of == lax.broadcasted_iota(jnp.int32, (block, 128), 1), 1.0, 0.0)
    to_ray = to_ray.astype(BF16)
    sample_of = lax.broadcasted_iota(jnp.int32, (SAMP, block), 1) & (SAMP - 1)
    own_row = sample_of == lax.broadcasted_iota(jnp.int32, (SAMP, block), 0)
    for j in range(rays // 128):
        part = sample_src[:, j * block : (j + 1) * block]
        pair = [(part >> 7).astype(F32), (part & 127).astype(F32)]
        pair = jnp.concatenate([jnp.where(own_row, p, 0.0) for p in pair], axis=0)
        got = matmul(pair.astype(BF16), to_ray)
        whole = got[:SAMP] * 128.0 + got[SAMP:]
        sources[:, j * 128 : (j + 1) * 128] = whole.astype(jnp.int32)

    sig_density = []
    intensity_here = []
    for b in range(nb):
        unfold(bricks[b].astype(F32), cols.at[b], lane)
        by_a = matmul(conv_rows, cols[b])
        pre = conv_b_col
        for a in range(3):
            pre = pre + moved(by_a[a * ch : (a + 1) * ch], 64, plane, a - 1)
        value, slope = gelu_and_slope(pre)
        feats = value.astype(BF16)
        decoded[b] = feats
        slope_conv[b] = slope
        x = matmul(w1_t, feats) + b1_col
        t = jnp.tanh(GELU_SCALE * (x + GELU_CUBIC * (x * (x * x))))
        hid_x[b] = x
        hid_t[b] = t
        value = x * (0.5 * (1.0 + t))
        e0 = jnp.sum(value * w2_density, axis=0, keepdims=True)
        e1 = jnp.sum(value * w2_intensity, axis=0, keepdims=True)
        density = jnp.maximum(e0, 0.0) + jnp.log1p(jnp.exp(-jnp.abs(e0)))
        sig_density.append(1.0 / (1.0 + jnp.exp(-e0)))
        intensity_here.append(1.0 / (1.0 + jnp.exp(-e1)))
        for h in range(halves):
            row = b * halves + h
            at = slice(h * 256, (h + 1) * 256)
            own_table[row : row + 1, :] = density[:, at]
            own_table[groups + row : groups + row + 1, :] = intensity_here[b][:, at]

    pl.semaphore_wait(barrier, count - 1)

    def give_table(k):
        return pltpu.make_async_remote_copy(
            src_ref=own_table,
            dst_ref=tables.at[sector],
            send_sem=table_sems.at[0, k],
            recv_sem=table_sems.at[1, k],
            device_id={"shell": shell, "sector": sector_after[k]},
            device_id_type=MESH,
        )

    for k in range(1, n):
        give_table(k).start()
    tables[sector] = own_table[...]

    asked = queries[...]
    parts = cap // 256
    asked = jnp.concatenate([asked[:, h * 256 : (h + 1) * 256] for h in range(parts)], axis=0)
    asked = jnp.concatenate([(asked >> 6).astype(F32), (asked & 63).astype(F32)], axis=0)
    asked = asked.astype(BF16)
    held = parts * n
    place_of = lax.broadcasted_iota(jnp.int32, (256, rays), 0)
    held_of = lax.broadcasted_iota(jnp.int32, (held, rays), 0)
    codes = []
    for k in range(SAMP):
        src = sources[k : k + 1, :]
        owner = src >> (cap.bit_length() - 1)
        got = matmul(asked, jnp.where(place_of == (src & 255), 1.0, 0.0).astype(BF16))
        got = got[:held] * 64.0 + got[held:]
        mine = held_of == ((src >> 8) & (parts - 1)) * n + owner
        address = jnp.sum(jnp.where(mine, got, 0.0), axis=0, keepdims=True).astype(jnp.int32)
        hot[k] = jnp.where(place_of == (address & 255), 1.0, 0.0).astype(BF16)
        codes.append(owner * groups + (address >> 8))

    for k in range(1, n):
        give_table(k).wait()

    everything = tables[...].reshape(n * 2 * groups, 256)
    everything = jnp.concatenate([p.astype(BF16) for p in split(everything, 2)], axis=1)
    group_of = lax.broadcasted_iota(jnp.int32, (groups, rays), 0)
    total = n * 2 * groups
    dens = []
    inten = []
    for k in range(SAMP):
        got = matmul(everything, jnp.concatenate([hot[k], hot[k]], axis=0))
        sums = [jnp.zeros((groups, rays), F32)] * 2
        for w in range(n):
            mine = group_of == codes[k] - w * groups
            for j in range(2):
                at = (2 * w + j) * groups
                sums[j] = sums[j] + jnp.where(mine, got[at : at + groups], 0.0)
        dens.append(jnp.sum(sums[0], axis=0, keepdims=True))
        inten.append(jnp.sum(sums[1], axis=0, keepdims=True))

    step_size = 2.0 / (shells * SAMP)
    span = 1.0 / (shells * SAMP)
    first = shell.astype(F32) * SAMP + 0.5
    before = jnp.zeros((1, rays), F32)
    depth = jnp.zeros((1, rays), F32)
    light = jnp.zeros((1, rays), F32)
    enter = []
    leave = []
    weight = []
    for k in range(SAMP):
        optical = dens[k] * step_size
        enter.append(jnp.exp(-before))
        leave.append(jnp.exp(-optical))
        weight.append(enter[k] * (1.0 - leave[k]))
        depth = depth + weight[k] * ((first + k) * span)
        light = light + weight[k] * inten[k]
        before = before + optical
    shell_buf[shell] = jnp.concatenate(
        [depth, light, before, jnp.zeros((5, rays), F32)], axis=0
    )

    def to_shell(k):
        return pltpu.make_async_remote_copy(
            src_ref=shell_buf.at[shell],
            dst_ref=shell_buf.at[shell],
            send_sem=shell_sems.at[0, k],
            recv_sem=shell_sems.at[1, k],
            device_id={"shell": shell_after[k], "sector": sector},
            device_id_type=MESH,
        )

    for k in range(1, shells):
        to_shell(k).start()
    for b in range(nb):
        x = hid_x[b]
        t = hid_t[b]
        half = 0.5 * (1.0 + t)
        hid_x[b] = x * half
        hid_t[b] = half + 0.5 * x * (1.0 - t * t) * (
            GELU_SCALE * (1.0 + 3.0 * GELU_CUBIC * (x * x))
        )

    for k in range(1, shells):
        to_shell(k).wait()

    prefix = jnp.zeros((1, rays), F32)
    ray_depth = jnp.zeros((1, rays), F32)
    ray_light = jnp.zeros((1, rays), F32)
    entry = []
    for s in range(shells):
        entry.append(jnp.exp(-prefix))
        ray_depth = ray_depth + entry[s] * shell_buf[s, 0:1, :]
        ray_light = ray_light + entry[s] * shell_buf[s, 1:2, :]
        prefix = prefix + shell_buf[s, 2:3, :]
    ray_depth_out[...] = ray_depth
    escape = jnp.exp(-prefix)
    dropped = drop_label[...].astype(F32)
    kept = 1.0 - dropped
    off_depth = ray_depth - depth_target[...]
    off_light = ray_light - inten_target[...]
    off_escape = escape - dropped
    loss = jnp.sum(
        kept * (off_depth * off_depth + off_light * off_light) + off_escape * off_escape,
        axis=1,
        keepdims=True,
    )
    grad_depth = 2.0 * kept * off_depth
    grad_light = 2.0 * kept * off_light
    behind = jnp.zeros((1, rays), F32)
    own_entry = jnp.zeros((1, rays), F32)
    for s in range(shells):
        term = (grad_depth * shell_buf[s, 0:1, :] + grad_light * shell_buf[s, 1:2, :]) * entry[s]
        behind = behind + jnp.where(shell < s, term, 0.0)
        own_entry = own_entry + jnp.where(shell == s, entry[s], 0.0)
    cot_depth = grad_depth * own_entry
    cot_light = grad_light * own_entry
    cot_tau = -2.0 * off_escape * escape - behind
    later = jnp.zeros((1, rays), F32)
    dens_grad = [None] * SAMP
    inten_grad = [None] * SAMP
    for k in reversed(range(SAMP)):
        pull = cot_depth * ((first + k) * span) + cot_light * inten[k]
        inten_grad[k] = cot_light * weight[k]
        dens_grad[k] = step_size * (pull * enter[k] * leave[k] - later + cot_tau)
        later = later + pull * weight[k]

    table_grad = jnp.zeros((2 * total, 256), F32)
    for k in range(SAMP):
        masks = [group_of == codes[k] - w * groups for w in range(n)]
        pair = [split(dens_grad[k], 2), split(inten_grad[k], 2)]
        spread = jnp.concatenate(
            [
                jnp.where(masks[w], pair[j][p], 0.0).astype(BF16)
                for p in range(2)
                for w in range(n)
                for j in range(2)
            ],
            axis=0,
        )
        table_grad = table_grad + matmul_nt(spread, hot[k])
    table_grad = table_grad[:total] + table_grad[total:]
    cell_send[...] = table_grad.reshape(n, 2 * groups, 256)

    def give_back(k):
        peer = sector_after[k]
        return pltpu.make_async_remote_copy(
            src_ref=cell_send.at[peer],
            dst_ref=cell_recv.at[sector],
            send_sem=cell_sems.at[0, k],
            recv_sem=cell_sems.at[1, k],
            device_id={"shell": shell, "sector": peer},
            device_id_type=MESH,
        )

    for k in range(1, n):
        give_back(k).start()
    cell_recv[sector] = cell_send[sector]
    w1_rep = matmul(w1[...], repeated_eye(hid, 3)).astype(BF16)
    turned = jnp.transpose(wide_w)
    back_rows = jnp.concatenate(
        [
            jnp.concatenate(
                [turned[(9 * a + 8 - k) * ch : (9 * a + 9 - k) * ch] for k in range(9)], axis=1
            )
            for a in range(3)
        ],
        axis=0,
    ).astype(BF16)
    for k in range(1, n):
        give_back(k).wait()
    table_grad = jnp.sum(cell_recv[...], axis=0)

    w1_acc = jnp.zeros((ch, 3 * hid), F32)
    small = [jnp.zeros((hid, 1), F32)] * 3
    wgrad = jnp.zeros((3 * ch, width), F32)
    bias_grad = jnp.zeros((ch, 1), F32)
    for b in range(nb):
        rows = [
            jnp.concatenate(
                [
                    table_grad[j * groups + b * halves + h : j * groups + b * halves + h + 1]
                    for h in range(halves)
                ],
                axis=1,
            )
            for j in range(2)
        ]
        g0 = rows[0] * sig_density[b]
        g1 = rows[1] * (intensity_here[b] * (1.0 - intensity_here[b]))
        value = hid_x[b]
        grad = (w2_density * g0 + w2_intensity * g1) * hid_t[b]
        pieces = jnp.concatenate([p.astype(BF16) for p in split(grad, 3)], axis=0)
        w1_acc = w1_acc + matmul_nt(decoded[b], pieces)
        terms = (grad, value * g0, value * g1)
        small = [a + jnp.sum(t, axis=1, keepdims=True) for a, t in zip(small, terms)]
        cot = (matmul(w1_rep, pieces) * slope_conv[b]).astype(BF16)
        exact = cot.astype(F32)
        cots[b] = cot
        by_a = [moved(exact, 64, plane, 1 - a).astype(BF16) for a in range(3)]
        wgrad = wgrad + matmul_nt(jnp.concatenate(by_a, axis=0), cols[b])
        bias_grad = bias_grad + jnp.sum(exact, axis=1, keepdims=True)

    tiles = -(-27 * ch // 128)
    wgrad = jnp.concatenate(
        [wgrad[a * ch : (a + 1) * ch] for a in range(3)]
        + [jnp.zeros((ch, tiles * 128 - 27 * ch), F32)],
        axis=1,
    )
    for t in range(tiles):
        for part in range(ch // 8):
            pack[t * (ch // 8) + part] = wgrad[part * 8 : part * 8 + 8, t * 128 : t * 128 + 128]
    at_lane = lax.broadcasted_iota(jnp.int32, (ch, 128), 1)
    w1_grad = w1_acc[:, :hid] + w1_acc[:, hid : 2 * hid] + w1_acc[:, 2 * hid :]
    last = jnp.concatenate([w1_grad, jnp.zeros((ch, 128 - hid), F32)], axis=1)
    place = hid
    for j in range(3):
        for part in range(hid // ch):
            values = small[j][part * ch : (part + 1) * ch, :]
            last = last + jnp.where(at_lane == place, values, 0.0)
            place += 1
    last = last + jnp.where(at_lane == place, bias_grad, 0.0)
    loss_here = jnp.where(shell == 0, loss, 0.0)
    last = last + jnp.where(at_lane == place + 1, loss_here, 0.0)
    base = tiles * (ch // 8)
    for part in range(ch // 8):
        pack[base + part] = last[part * 8 : part * 8 + 8]
    for extra in range(base + ch // 8, pack.shape[0]):
        pack[extra] = jnp.zeros((8, 128), F32)

    def to_reducer(k):
        peer, where = flat_peer(k)
        return pltpu.make_async_remote_copy(
            src_ref=pack.at[peer],
            dst_ref=red_recv.at[me],
            send_sem=red_sems.at[0, k],
            recv_sem=red_sems.at[1, k],
            device_id=where,
            device_id_type=MESH,
        )

    def to_everyone(k):
        _, where = flat_peer(k)
        return pltpu.make_async_remote_copy(
            src_ref=reduced.at[me],
            dst_ref=reduced.at[me],
            send_sem=out_sems.at[0, k],
            recv_sem=out_sems.at[1, k],
            device_id=where,
            device_id_type=MESH,
        )

    for k in range(1, count):
        to_reducer(k).start()

    red_recv[me] = pack[me]

    def brick_back(b):
        unfold(cots[b].astype(F32), cot_cols.at[b], lane)
        by_a = matmul(back_rows, cot_cols[b])
        grad = jnp.zeros((ch, cells), F32)
        for a in range(3):
            grad = grad + moved(by_a[a * ch : (a + 1) * ch], 64, plane, 1 - a)
        grad_bricks[b] = grad.astype(BF16)

    for b in range(nb // 2):
        brick_back(b)

    for k in range(1, count):
        to_reducer(k).wait()

    reduced[me] = jnp.sum(red_recv[...], axis=0)

    for k in range(1, count):
        to_everyone(k).start()

    for b in range(nb // 2, nb):
        brick_back(b)

    for k in range(1, count):
        to_everyone(k).wait()


def finish(
    scale,
    reduced,
    grad_bricks,
    ray_depth,
    loss_out,
    conv_out,
    conv_b_out,
    w1_out,
    b1_out,
    w2_out,
    bricks_out,
    depth_out,
):
    ch, used = conv_out.shape
    hid = w1_out.shape[1]
    per = ch // 8
    tiles = -(-used // 128)
    for t in range(tiles):
        stop = min(128, used - t * 128)
        for part in range(per):
            conv_out[part * 8 : part * 8 + 8, t * 128 : t * 128 + stop] = reduced[
                t * per + part, :, :stop
            ]
    last = jnp.concatenate([reduced[tiles * per + part] for part in range(per)], axis=0)
    w1_out[...] = last[:, :hid]

    def row(place, count):
        i = lax.broadcasted_iota(jnp.int32, (ch, ch * count), 0)
        j = lax.broadcasted_iota(jnp.int32, (ch, ch * count), 1)
        total = jnp.zeros((1, ch * count), F32)
        for part in range(count):
            spread = jnp.where(j == i + part * ch, last[:, place + part : place + part + 1], 0.0)
            total = total + jnp.sum(spread, axis=0, keepdims=True)
        return total

    count = hid // ch
    b1_out[...] = row(hid, count)
    w2_out[0:1, :] = row(hid + count, count)
    w2_out[1:2, :] = row(hid + 2 * count, count)
    place = hid + 3 * count
    conv_b_out[...] = row(place, 1)
    loss_out[...] = last[0:1, place + 1 : place + 2] * scale
    bricks_out[...] = grad_bricks[...]
    depth_out[...] = ray_depth[...]


def local(
    bricks,
    conv_w,
    conv_b,
    head_w1,
    head_b1,
    head_w2,
    queries,
    sample_src,
    depth_target,
    inten_target,
    drop_label,
):
    shells = lax.axis_size("shell")
    n = lax.axis_size("sector")
    count = shells * n
    _, nb, ch, cells = bricks.shape
    cap = queries.shape[2]
    hid = head_w1.shape[1]
    rays = depth_target.shape[0]
    groups = nb * cells // 256
    chunks = (-(-27 * ch // 128) + 1) * (ch // 8)
    assert chunks <= count and cap & (cap - 1) == 0 and cap >= 256 and cells == 512 and rays % 128 == 0
    operands = (
        bricks[0],
        conv_w,
        conv_b[None],
        head_w1,
        head_b1[None],
        head_w2.T,
        queries[0],
        sample_src,
        depth_target[None],
        inten_target[None],
        drop_label[None],
    )
    vmem = pl.BlockSpec(memory_space=pltpu.VMEM)
    dma = pltpu.SemaphoreType.DMA
    grad_bricks, ray_depth, reduced = pl.pallas_call(
        functools.partial(body, shells, n),
        out_shape=(
            jax.ShapeDtypeStruct((nb, ch, cells), BF16),
            jax.ShapeDtypeStruct((1, rays), F32),
            jax.ShapeDtypeStruct((count, 8, 128), F32),
        ),
        in_specs=[vmem] * len(operands),
        out_specs=(vmem, vmem, vmem),
        scratch_shapes=[
            pltpu.VMEM((SAMP, rays), jnp.int32),
            pltpu.VMEM((nb, ch, cells), BF16),
            pltpu.VMEM((nb, ch, cells), F32),
            pltpu.VMEM((nb, 9 * ch, cells), BF16),
            pltpu.VMEM((nb, 9 * ch, cells), BF16),
            pltpu.VMEM((nb, ch, cells), BF16),
            pltpu.VMEM((SAMP, 256, rays), BF16),
            pltpu.VMEM((nb, hid, cells), F32),
            pltpu.VMEM((nb, hid, cells), F32),
            pltpu.VMEM((2 * groups, 256), F32),
            pltpu.VMEM((n, 2 * groups, 256), F32),
            pltpu.VMEM((shells, 8, rays), F32),
            pltpu.VMEM((n, 2 * groups, 256), F32),
            pltpu.VMEM((n, 2 * groups, 256), F32),
            pltpu.VMEM((count, 8, 128), F32),
            pltpu.VMEM((count, 8, 128), F32),
            dma((2, n)),
            dma((2, shells)),
            dma((2, n)),
            dma((2, count)),
            dma((2, count)),
        ],
        compiler_params=pltpu.CompilerParams(
            collective_id=0, has_side_effects=True, vmem_limit_bytes=56 * 1024 * 1024
        ),
    )(*operands)
    loss, conv_grad, conv_b_grad, w1_grad, b1_grad, w2_grad, grad_bricks, ray_depth = pl.pallas_call(
        functools.partial(finish, 1.0 / (rays * n)),
        out_shape=(
            jax.ShapeDtypeStruct((1, 1), F32),
            jax.ShapeDtypeStruct((ch, 27 * ch), F32),
            jax.ShapeDtypeStruct((1, ch), F32),
            jax.ShapeDtypeStruct((ch, hid), F32),
            jax.ShapeDtypeStruct((1, hid), F32),
            jax.ShapeDtypeStruct((2, hid), F32),
            jax.ShapeDtypeStruct((nb, ch, cells), BF16),
            jax.ShapeDtypeStruct((1, rays), F32),
        ),
        in_specs=[vmem] * 3,
        out_specs=(vmem,) * 8,
    )(reduced, grad_bricks, ray_depth)
    return (
        loss[0, 0],
        conv_grad,
        conv_b_grad[0],
        w1_grad,
        b1_grad[0],
        w2_grad.T,
        grad_bricks[None],
        ray_depth[0],
    )


def solution(mesh):
    return jax.shard_map(
        local,
        mesh=mesh,
        in_specs=(
            P("shell", "sector", None, None),
            P(),
            P(),
            P(),
            P(),
            P(),
            P("shell", "sector", None),
            P("shell", "sector"),
            P("sector"),
            P("sector"),
            P("sector"),
        ),
        out_specs=(P(), P(), P(), P(), P(), P(), P("shell", "sector", None, None), P("sector")),
        check_vma=False,
    )
```
